128 devices in a mesh: row: 8 (over x_lo, y), col: 16 (over z, x_hi, core).
Axes of the slice: x: 4 (x_hi: 2, x_lo: 2; x = x_hi * 2 + x_lo), y: 4, z: 4, core: 2. Of those that a mesh axis runs over, the one named last changes fastest.
Arguments:
- pair: float32 [256, 256, 128], P('row', 'col'), may hold values from -6 to 6
- cotangent: float32 [256, 256, 128], P('row', 'col'), may hold values from -6 to 6
- tri_bias: float32 [4, 256, 256], P(None, 'col'), may hold values from -4 to 400
- valid_length: int32 [1], replicated, may hold values from 128 to 256
- gain_first: float32 [128], replicated, may hold values from 0.25 to 1.75
- w_first: float32 [128, 640], replicated, may hold values from -0.5 to 0.5
- gain_mid: float32 [128], replicated, may hold values from 0.25 to 1.75
- w_mid: float32 [128, 128], replicated, may hold values from -0.5 to 0.5
- gain_second: float32 [128], replicated, may hold values from 0.25 to 1.75
- w_second: float32 [128, 512], replicated, may hold values from -0.5 to 0.5
- w_att_out: float32 [128, 128], replicated, may hold values from -0.5 to 0.5
Outputs:
- pair_out: float32 [256, 256, 128], P('row', 'col')
- pair_grad: float32 [256, 256, 128], P('row', 'col')
The draws below stay inside these ranges and needn't reach their ends.
All inputs are finite; a program needn't handle non-finite values.
Results may differ from the reference program's by a relative error of at most 0.0003.
Values sent between devices are 32-bit elements; how exact they have to be, the bound alone decides.
A program may use at most 128 MiB of HBM per device.

```python
import jax
import jax.numpy as jnp
from jax import lax

C = 128
MULT = 128
HEADS = 4
ATT = 128
TOKENS = 256


def draw_tri_bias(key, part):
    key = jax.random.fold_in(key, 11)
    key_base = jax.random.fold_in(key, 0)
    shape = (HEADS, TOKENS, TOKENS)
    return jnp.clip(jax.random.normal(key_base, shape, jnp.float32), -4.0, 4.0)


def shard_levels(rng, extent, shards, low, top_value):
    level = 1.0
    for dim, parts in shards:
        heights = jax.random.uniform(jax.random.fold_in(jax.random.fold_in(rng, 6), dim), (parts,), jnp.float32, low / len(shards), top_value / len(shards))
        level = level * jnp.repeat(jnp.exp(heights), extent[dim] // parts).reshape((-1,) + (1,) * (len(extent) - 1 - dim))
    return level


def noise(stream_key, shape, scale, limit, cuts=(), held_as=jnp.bfloat16):
    values = scale * jax.random.normal(stream_key, shape, jnp.float32)
    if cuts:
        values = values * shard_levels(stream_key, shape, cuts, -0.22, 0.18)
    return jnp.clip(values, -limit, limit).astype(held_as)


def setup_inputs(seed: int = 0) -> dict:
    arg_keys = jax.random.split(jax.random.key(seed), 12)
    pair = noise(arg_keys[0], (TOKENS, TOKENS, C), 1.0, 6.0, ((0, 8), (1, 16)), jnp.float32)
    cotangent = noise(arg_keys[1], (TOKENS, TOKENS, C), 1.0, 6.0, ((0, 8), (1, 16)), jnp.float32)
    tri_bias = draw_tri_bias(jax.random.fold_in(arg_keys[11], 71), 0)
    valid_length = jax.random.randint(arg_keys[3], (1,), TOKENS // 2, TOKENS + 1).astype(jnp.int32)
    gain_first = jnp.clip(1.0 + 0.15 * jax.random.normal(arg_keys[4], (C,), jnp.float32), 0.25, 1.75)
    w_first = noise(arg_keys[5], (C, 4 * MULT + C), C ** -0.5, 0.5, (), jnp.float32)
    gain_mid = jnp.clip(1.0 + 0.15 * jax.random.normal(arg_keys[6], (MULT,), jnp.float32), 0.25, 1.75)
    w_mid = noise(arg_keys[7], (MULT, C), MULT ** -0.5, 0.5, (), jnp.float32)
    gain_second = jnp.clip(1.0 + 0.15 * jax.random.normal(arg_keys[8], (C,), jnp.float32), 0.25, 1.75)
    w_second = noise(arg_keys[9], (C, 4 * ATT), C ** -0.5, 0.5, (), jnp.float32)
    w_att_out = noise(arg_keys[10], (ATT, C), ATT ** -0.5, 0.5, (), jnp.float32)
    return dict(pair=pair, cotangent=cotangent, tri_bias=tri_bias, valid_length=valid_length, gain_first=gain_first, w_first=w_first, gain_mid=gain_mid, w_mid=w_mid, gain_second=gain_second, w_second=w_second, w_att_out=w_att_out)


EPSILON = 1e-05
MASK_SHIFT = 1000000000.0
HIGHEST_PRECISION = lax.Precision.HIGHEST

def layer_norm(values, gain_vector):
    centre = values - lax.optimization_barrier(jnp.mean(values, axis=-1, keepdims=True))
    spread = lax.optimization_barrier(jnp.mean(centre * centre, axis=-1, keepdims=True))
    return centre * lax.rsqrt(spread + EPSILON) * gain_vector

def project(values, weight):
    return jnp.einsum('ijc,cd->ijd', values, weight, precision=HIGHEST_PRECISION)

def forward(pair, tri_bias, valid_length, gain_first, w_first, gain_mid, w_mid, gain_second, w_second, w_att_out):
    token_count = pair.shape[0]
    mult_width = w_mid.shape[0]
    att_width = w_att_out.shape[0]
    head_count = tri_bias.shape[0]
    head_width = att_width // head_count
    valid_mask = (jnp.arange(token_count) < valid_length[0]).astype(jnp.float32)
    pair_mask = (valid_mask[:, None] * valid_mask[None, :])[:, :, None]
    projected = project(layer_norm(pair, gain_first), w_first)
    left_factor = pair_mask * jax.nn.sigmoid(projected[..., :mult_width]) * projected[..., mult_width:2 * mult_width]
    right_factor = pair_mask * jax.nn.sigmoid(projected[..., 2 * mult_width:3 * mult_width]) * projected[..., 3 * mult_width:4 * mult_width]
    out_gate = jax.nn.sigmoid(projected[..., 4 * mult_width:])
    product = jnp.einsum('ikc,jkc->ijc', left_factor, right_factor, precision=HIGHEST_PRECISION)
    middle = pair + out_gate * project(layer_norm(product, gain_mid), w_mid)
    second = project(layer_norm(middle, gain_second), w_second)
    query = second[..., :att_width]
    key_all = second[..., att_width:2 * att_width]
    value_all = second[..., 2 * att_width:3 * att_width]
    att_gate = jax.nn.sigmoid(second[..., 3 * att_width:])
    key_shift = (valid_mask - 1.0) * MASK_SHIFT
    score_scale = 1.0 / jnp.sqrt(jnp.float32(head_width))

    def attend_row(inputs):
        query_row, key_row, value_row = inputs
        query_heads = query_row.reshape(token_count, head_count, head_width)
        key_heads = key_row.reshape(token_count, head_count, head_width)
        value_heads = value_row.reshape(token_count, head_count, head_width)
        scores = jnp.einsum('jhd,khd->hjk', query_heads, key_heads, precision=HIGHEST_PRECISION) * score_scale
        scores = scores + tri_bias + key_shift[None, None, :]
        weights = jax.nn.softmax(scores, axis=-1)
        attended = jnp.einsum('hjk,khd->jhd', weights, value_heads, precision=HIGHEST_PRECISION)
        return attended.reshape(token_count, att_width)
    attended = lax.map(attend_row, (query, key_all, value_all))
    return middle + project(att_gate * attended, w_att_out)

def reference(pair, cotangent, tri_bias, valid_length, gain_first, w_first, gain_mid, w_mid, gain_second, w_second, w_att_out):

    def apply_layer(values):
        return forward(values, tri_bias, valid_length, gain_first, w_first, gain_mid, w_mid, gain_second, w_second, w_att_out)
    pair_out, pull_back = jax.vjp(apply_layer, pair)
    pair_grad, = pull_back(cotangent)
    return (pair_out, pair_grad)
```

```python
import functools
import math

import jax
import jax.numpy as jnp
from jax import lax
from jax.experimental import pallas as pl
from jax.experimental.pallas import tpu as pltpu
from jax.sharding import PartitionSpec as P

EPSILON = 1e-05
MASK_SHIFT = 1000000000.0
MESH = pl.DeviceIdType.MESH
F32 = jnp.float32
BF16 = jnp.bfloat16
NN = (((1,), (0,)), ((), ()))
NT = (((1,), (1,)), ((), ()))

T = 256
C = 128
HEADS = 4
WIDTH = 32
ROWS = 8
COLS = 16
N = ROWS * COLS
TI = T // ROWS
TJ = T // COLS
POS = TI * TJ
OWN = T // N


def split(x):
    hi = x.astype(BF16)
    return hi, (x - hi.astype(F32)).astype(BF16)


def dot(a, b, dims=NN):
    return lax.dot_general(a, b, dims, preferred_element_type=F32)


def mm(a, b, dims=NN):
    return dot(a[0], b[0], dims) + (dot(a[0], b[1], dims) + dot(a[1], b[0], dims))


def norm(u):
    centre = u - jnp.mean(u, axis=-1, keepdims=True)
    scale = lax.rsqrt(jnp.mean(centre * centre, axis=-1, keepdims=True) + EPSILON)
    return centre * scale, scale


def norm_back(d, xhat, scale):
    mean_d = jnp.mean(d, axis=-1, keepdims=True)
    mean_dx = jnp.mean(d * xhat, axis=-1, keepdims=True)
    return scale * (d - mean_d - xhat * mean_dx)


def swap_blocks(xs):
    block = lax.broadcasted_iota(jnp.int32, xs[0].shape, 1) // 32
    for bit in (2, 1):
        upper = (block & bit) != 0
        ys = list(xs)
        for s in range(4):
            if s & bit == 0:
                a, b = xs[s], xs[s | bit]
                ys[s] = jnp.where(upper, pltpu.roll(b, 32 * bit, 1), a)
                ys[s | bit] = jnp.where(upper, b, pltpu.roll(a, 128 - 32 * bit, 1))
        xs = ys
    return xs


def head_rows(x, h):
    zero = jnp.zeros((WIDTH, x.shape[1]), x.dtype)
    return jnp.concatenate([x[WIDTH * h : WIDTH * (h + 1)] if g == h else zero for g in range(HEADS)], axis=0)


def kernel(
    valid_ref,
    pair_ref,
    cot_ref,
    bias_ref,
    gain_first,
    w_first,
    gain_mid,
    w_mid,
    gain_second,
    w_second,
    w_att_out,
    out_ref,
    grad_ref,
    send_a,
    recv_a,
    send_x,
    recv_x,
    send_d,
    recv_d,
    send_g,
    recv_g,
    pair_r,
    cot_r,
    bias_r,
    bias_t,
    out_r,
    grad_r,
    grad_t,
    xhat_t,
    scale_t,
    proj_t,
    mask_t,
    at_s,
    bt_s,
    at_hi,
    at_lo,
    bt_hi,
    bt_lo,
    dx_s,
    e_hi,
    e_lo,
    ph_r,
    ps_r,
    g1_r,
    dgated_r,
    sem_in,
    a_sems,
    x_sems,
    d_sems,
    g_sems,
    pair_sems,
    cot_sems,
    bias_sems,
    out_sems,
    grad_sems,
):
    r = lax.axis_index("row")
    c = lax.axis_index("col")
    me = r * COLS + c
    valid = valid_ref[0]

    barrier = pltpu.get_barrier_semaphore()

    def greet_col(i, _):
        pl.semaphore_signal(barrier, inc=1, device_id=(r, lax.rem(c + i, COLS)), device_id_type=MESH)
        return 0

    def greet_row(i, _):
        pl.semaphore_signal(barrier, inc=1, device_id=(lax.rem(r + i, ROWS), c), device_id_type=MESH)
        return 0

    lax.fori_loop(1, COLS, greet_col, 0)
    lax.fori_loop(1, ROWS, greet_row, 0)

    def send_all(src, dst, sems):
        def go(i, _):
            d = lax.rem(me + i, N)
            pltpu.make_async_remote_copy(
                src(d), dst, sems.at[0], sems.at[1], device_id=(d // COLS, lax.rem(d, COLS)), device_id_type=MESH
            ).start()
            return 0

        lax.fori_loop(1, N, go, 0)

    def send_cols(src, dst, sems):
        def go(i, _):
            d = lax.rem(c + i, COLS)
            pltpu.make_async_remote_copy(
                src(d), dst, sems.at[0], sems.at[1], device_id=(r, d), device_id_type=MESH
            ).start()
            return 0

        lax.fori_loop(1, COLS, go, 0)

    def waiter(view, sems):
        return pltpu.make_async_remote_copy(view, view, sems.at[0], sems.at[1], device_id=(r, c), device_id_type=MESH)

    pair_flat = pair_ref.reshape(POS, C)
    u = jnp.concatenate([pair_flat[pl.ds(kk, TI, stride=TJ)] for kk in range(TJ)], axis=0)
    xhat, scale = norm(u)
    xhat_t[...] = xhat
    scale_t[...] = jnp.broadcast_to(scale, (POS, C))
    w03 = split(w_first[:, : 4 * C])
    proj = mm(split(xhat * gain_first[...]), w03)
    pos = lax.broadcasted_iota(jnp.int32, (POS, C), 0)
    in_row = (r * TI + pos % TI) < valid
    in_col = (c * TJ + pos // TI) < valid
    mask = jnp.where(in_row & in_col, 1.0, 0.0).astype(F32)
    mask_t[...] = mask
    sig0 = jax.nn.sigmoid(proj[:, :C])
    sig2 = jax.nn.sigmoid(proj[:, 2 * C : 3 * C])
    p1 = proj[:, C : 2 * C]
    p3 = proj[:, 3 * C :]
    proj_t[0] = sig0
    proj_t[1] = p1
    proj_t[2] = sig2
    proj_t[3] = p3
    left = mask * sig0 * p1
    right = mask * sig2 * p3
    sa = send_a.reshape(N * 8, C)
    for q in range(4):
        sa[pl.ds(q, C, stride=8)] = left[128 * q : 128 * (q + 1)].T
        sa[pl.ds(4 + q, C, stride=8)] = right[128 * q : 128 * (q + 1)].T

    pl.semaphore_wait(barrier, COLS - 1 + ROWS - 1)

    def greet_again(i, _):
        pl.semaphore_signal(sem_in, inc=1, device_id=(lax.rem(r + i, ROWS), c), device_id_type=MESH)
        return 0

    lax.fori_loop(1, ROWS, greet_again, 0)
    pl.semaphore_wait(sem_in, ROWS - 1)

    send_all(lambda d: send_a.at[d], recv_a.at[me], a_sems)
    recv_a[me] = send_a[me]

    pair_view = pair_ref.reshape(OWN, TJ, TJ, C)
    cot_view = cot_ref.reshape(OWN, TJ, TJ, C)
    here = pl.ds(pl.multiple_of(c * TJ, TJ), TJ)
    send_cols(lambda d: pair_view.at[:, d], pair_r.at[:, here], pair_sems)
    send_cols(lambda d: cot_view.at[:, d], cot_r.at[:, here], cot_sems)
    send_cols(lambda d: bias_ref, bias_r.at[:, here], bias_sems)
    pair_r[:, here] = pair_view[:, c]
    cot_r[:, here] = cot_view[:, c]
    bias_r[:, here] = bias_ref[...]

    waiter(recv_a.at[pl.ds(0, N - 1)], a_sems).wait_recv()
    ra = recv_a.reshape(N * 8, C)
    for part, dest in ((0, at_s), (4, bt_s)):
        for half in range(2):
            for q in range(4):
                ys = swap_blocks(
                    [ra[pl.ds((64 * half + 16 * rr) * 8 + part + q, COLS, stride=8)] for rr in range(4)]
                )
                for g in range(4):
                    dest[pl.ds((4 * q + g) * COLS, COLS), pl.ds(128 * half, 128)] = ys[g]
    at = at_s[...]
    a_parts = split(at.T)
    at_parts = split(at)
    at_hi[...], at_lo[...] = at_parts
    bt_parts = split(bt_s[...])
    bt_hi[...], bt_lo[...] = bt_parts
    x = mm(a_parts, bt_parts)
    for l in range(OWN):
        sx = send_x.at[l].reshape(N * 8, C)
        for rr in range(ROWS):
            for jh in range(2):
                sx[pl.ds(16 * rr * 8 + jh, COLS, stride=8)] = x[
                    TI * rr + 16 * l : TI * rr + 16 * (l + 1), 128 * jh : 128 * (jh + 1)
                ]
        send_all(lambda d: send_x.at[l, d, pl.ds(0, 2)], recv_x.at[l, me, pl.ds(0, 2)], x_sems.at[l])
        recv_x[l, me] = send_x[l, me]

    waiter(pair_r.reshape(OWN * T, C).at[pl.ds(0, OWN * TJ * (COLS - 1))], pair_sems).wait_recv()
    waiter(cot_r.reshape(OWN * T, C).at[pl.ds(0, OWN * TJ * (COLS - 1))], cot_sems).wait_recv()
    w4 = split(w_first[:, 4 * C :])
    w_out = split(w_att_out[...])
    for l in range(OWN):
        ph, ps = norm(pair_r[l])
        ph_r[l] = ph
        ps_r[l] = jnp.broadcast_to(ps, (T, C))
        g1_r[l] = jax.nn.sigmoid(mm(split(ph * gain_first[...]), w4))
        dgated_r[l] = mm(split(cot_r[l]), w_out, NT)
    waiter(bias_r.reshape(HEADS * T, T).at[pl.ds(0, HEADS * TJ * (COLS - 1))], bias_sems).wait_recv()
    key = lax.broadcasted_iota(jnp.int32, (T, T), 0)
    shift = jnp.where(key < valid, 0.0, -MASK_SHIFT).astype(F32)
    for h in range(HEADS):
        bias_t[h] = bias_r[h].T + shift

    w_sec = split(w_second[...])
    w_m = split(w_mid[...])
    score_scale = 1.0 / math.sqrt(WIDTH)

    def row(l, _):
        waiter(recv_x.at[l, pl.ds(0, N - 1), pl.ds(0, 2)], x_sems.at[l]).wait_recv()
        rx = recv_x.at[l].reshape(N * 8, C)
        x = jnp.concatenate([rx[pl.ds(jh, C, stride=8)].T for jh in range(2)], axis=0)
        xh, xs = norm(x)
        m = mm(split(xh * gain_mid[...]), w_m)
        g1 = g1_r[l]
        z1 = pair_r[l] + g1 * m
        zh, zs = norm(z1)
        second = mm(split(zh * gain_second[...]), w_sec)
        q = second[:, :C] * score_scale
        k = second[:, C : 2 * C]
        v = second[:, 2 * C : 3 * C]
        g2 = jax.nn.sigmoid(second[:, 3 * C :])
        k_hi, k_lo = split(k)
        v_hi, v_lo = split(v)
        q_hi, q_lo = split(q)
        qt_hi, qt_lo = split(q.T)
        kt_hi, kt_lo = split(k.T)
        vt_hi, vt_lo = split(v.T)
        k_both = jnp.concatenate([k_hi, k_lo], axis=1)
        v_both = jnp.concatenate([v_hi, v_lo], axis=1)
        ots = []
        inverses = []
        for h in range(HEADS):
            hs = slice(WIDTH * h, WIDTH * (h + 1))
            top = head_rows(qt_hi, h)
            s = dot(k_both, jnp.concatenate([top, top], axis=0)) + dot(k_hi, head_rows(qt_lo, h))
            s = s + bias_t[h]
            e = jnp.exp(s - jnp.max(s, axis=0, keepdims=True))
            inverse = 1.0 / jnp.sum(e, axis=0, keepdims=True)
            eh, el = split(e)
            e_hi[h] = eh
            e_lo[h] = el
            both = dot(jnp.concatenate([vt_hi[hs], vt_lo[hs]], axis=0), eh)
            ot = both[:WIDTH] + (both[WIDTH:] + dot(vt_hi[hs], el))
            ots.append(ot * inverse)
            inverses.append(inverse)
        ot = jnp.concatenate(ots, axis=0)
        o = ot.T
        out_r[l] = z1 + mm(split(g2 * o), w_out)
        send_cols(
            lambda d: out_r.at[l, pl.ds(pl.multiple_of(d * TJ, TJ), TJ)], out_ref.at[l * TJ + c], out_sems.at[l]
        )
        out_ref[l * TJ + c] = out_r[l, here]

        dgated = dgated_r[l]
        d_o = dgated * g2
        d_s = dgated * o * g2 * (1.0 - g2)
        d_ot = d_o.T
        d_ots = []
        deltas = []
        for h in range(HEADS):
            hs = slice(WIDTH * h, WIDTH * (h + 1))
            part = d_ot[hs] * inverses[h]
            deltas.append(jnp.sum(part * ots[h], axis=0, keepdims=True))
            d_ots.append(part)
        d_ots = jnp.concatenate(d_ots, axis=0)
        d_os_hi, d_os_lo = split(d_ots.T)
        dt_hi, dt_lo = split(d_ots)
        lane = lax.broadcasted_iota(jnp.int32, (T, C), 1) // WIDTH
        zero = jnp.zeros((T, C), BF16)
        dk = jnp.zeros((T, 2 * C), F32)
        dv = jnp.zeros((T, 2 * C), F32)
        dk_low = jnp.zeros((T, C), F32)
        dv_low = jnp.zeros((T, C), F32)
        dqs = []
        for h in range(HEADS):
            hs = slice(WIDTH * h, WIDTH * (h + 1))
            own = lane == h
            top = head_rows(dt_hi, h)
            dp = dot(v_both, jnp.concatenate([top, top], axis=0)) + dot(v_hi, head_rows(dt_lo, h))
            eh = e_hi[h]
            el = e_lo[h]
            ds = (eh.astype(F32) + el.astype(F32)) * (dp - deltas[h])
            dsh, dsl = split(ds)
            both = dot(jnp.concatenate([kt_hi[hs], kt_lo[hs]], axis=0), dsh)
            dqs.append(both[:WIDTH] + (both[WIDTH:] + dot(kt_hi[hs], dsl)))
            qm_hi = jnp.where(own, q_hi, zero)
            qm_lo = jnp.where(own, q_lo, zero)
            dk = dk + dot(dsh, jnp.concatenate([qm_hi, qm_lo], axis=1))
            dk_low = dk_low + dot(dsl, qm_hi)
            om_hi = jnp.where(own, d_os_hi, zero)
            om_lo = jnp.where(own, d_os_lo, zero)
            dv = dv + dot(eh, jnp.concatenate([om_hi, om_lo], axis=1))
            dv_low = dv_low + dot(el, om_hi)
        dq = jnp.concatenate(dqs, axis=0).T * score_scale
        dk = dk[:, :C] + (dk[:, C:] + dk_low)
        dv = dv[:, :C] + (dv[:, C:] + dv_low)
        d_second = jnp.concatenate([dq, dk, dv, d_s], axis=1)
        du2 = mm(split(d_second), w_sec, NT) * gain_second[...]
        dz1 = cot_r[l] + norm_back(du2, zh, zs)
        du = mm(split(dz1 * g1), w_m, NT) * gain_mid[...]
        dx = norm_back(du, xh, xs)
        sd = send_d.at[l].reshape(N * 8, C)
        for jh in range(2):
            sd[pl.ds(jh, C, stride=8)] = dx[128 * jh : 128 * (jh + 1)].T
        send_all(lambda d: send_d.at[l, d, pl.ds(0, 2)], recv_d.at[l, me, pl.ds(0, 2)], d_sems.at[l])
        recv_d[l, me] = send_d[l, me]
        dp4 = dz1 * m * g1 * (1.0 - g1)
        grad_r[l] = dz1 + norm_back(mm(split(dp4), w4, NT) * gain_first[...], ph_r[l], ps_r[l])
        send_cols(
            lambda d: grad_r.at[l, pl.ds(pl.multiple_of(d * TJ, TJ), TJ)], grad_t.at[l * TJ + c], grad_sems.at[l]
        )
        grad_t[l * TJ + c] = grad_r[l, here]
        return 0

    lax.fori_loop(0, OWN, row, 0)

    for l in range(OWN):
        waiter(recv_d.at[l, pl.ds(0, N - 1), pl.ds(0, 2)], d_sems.at[l]).wait_recv()
        rd = recv_d.at[l].reshape(N * 8, C)
        for rr in range(ROWS):
            for jh in range(2):
                dx_s[pl.ds(TI * rr + 16 * l, 16), pl.ds(128 * jh, 128)] = rd[pl.ds(16 * rr * 8 + jh, COLS, stride=8)]
    dx_parts = split(dx_s[...])
    d_bt = mm((at_hi[...], at_lo[...]), dx_parts)
    d_at = mm((bt_hi[...], bt_lo[...]), dx_parts, NT)
    sg = send_g.reshape(N * 8, C)
    for part, d_src in ((0, d_at), (4, d_bt)):
        for half in range(2):
            for q in range(4):
                ys = swap_blocks(
                    [
                        d_src[(4 * q + g) * COLS : (4 * q + g + 1) * COLS, 128 * half : 128 * (half + 1)]
                        for g in range(4)
                    ]
                )
                for rr in range(4):
                    sg[pl.ds((64 * half + 16 * rr) * 8 + part + q, COLS, stride=8)] = ys[rr]
    send_all(lambda d: send_g.at[d], recv_g.at[me], g_sems)
    recv_g[me] = send_g[me]

    waiter(recv_g.at[pl.ds(0, N - 1)], g_sems).wait_recv()
    rg = recv_g.reshape(N * 8, C)
    mask = mask_t[...]
    da = jnp.concatenate([rg[pl.ds(q, C, stride=8)].T for q in range(4)], axis=0) * mask
    db = jnp.concatenate([rg[pl.ds(4 + q, C, stride=8)].T for q in range(4)], axis=0) * mask
    sig0 = proj_t[0]
    sig2 = proj_t[2]
    dp1 = da * sig0
    dp3 = db * sig2
    dp0 = dp1 * proj_t[1] * (1.0 - sig0)
    dp2 = dp3 * proj_t[3] * (1.0 - sig2)
    d_proj = jnp.concatenate([dp0, dp1, dp2, dp3], axis=1)
    w03 = split(w_first[:, : 4 * C])
    du = mm(split(d_proj), w03, NT) * gain_first[...]
    res = norm_back(du, xhat_t[...], scale_t[...])
    grad_flat = grad_ref.reshape(POS, C)
    part_flat = grad_t.reshape(POS, C)
    for l in range(OWN):
        waiter(grad_t.at[pl.ds(0, COLS - 1)], grad_sems.at[l]).wait_recv()
    for kk in range(TJ):
        grad_flat[pl.ds(kk, TI, stride=TJ)] = res[TI * kk : TI * (kk + 1)] + part_flat[pl.ds(kk, TI, stride=TJ)]

    waiter(recv_a.at[pl.ds(0, N - 1)], a_sems).wait_send()
    waiter(pair_r.reshape(OWN * T, C).at[pl.ds(0, OWN * TJ * (COLS - 1))], pair_sems).wait_send()
    waiter(cot_r.reshape(OWN * T, C).at[pl.ds(0, OWN * TJ * (COLS - 1))], cot_sems).wait_send()
    waiter(bias_r.reshape(HEADS * T, T).at[pl.ds(0, HEADS * TJ * (COLS - 1))], bias_sems).wait_send()
    waiter(recv_g.at[pl.ds(0, N - 1)], g_sems).wait_send()
    for l in range(OWN):
        waiter(recv_x.at[l, pl.ds(0, N - 1), pl.ds(0, 2)], x_sems.at[l]).wait_send()
        waiter(recv_d.at[l, pl.ds(0, N - 1), pl.ds(0, 2)], d_sems.at[l]).wait_send()
        waiter(grad_t.at[pl.ds(0, COLS - 1)], grad_sems.at[l]).wait_send()
        waiter(out_ref.at[pl.ds(0, COLS - 1)], out_sems.at[l]).wait()


def body(pair, cotangent, tri_bias, valid_length, gain_first, w_first, gain_mid, w_mid, gain_second, w_second, w_att_out):
    vmem = pl.BlockSpec(memory_space=pltpu.VMEM)
    smem = pl.BlockSpec(memory_space=pltpu.SMEM)
    tile = jax.ShapeDtypeStruct((TI, TJ, C), F32)
    message = pltpu.VMEM((N, 8, C), F32)
    halves = pltpu.VMEM((OWN, N, 8, C), F32)
    rows = pltpu.VMEM((OWN, T, C), F32)
    square = pltpu.VMEM((T, T), F32)
    square_low = pltpu.VMEM((T, T), BF16)
    pair_of = pltpu.SemaphoreType.DMA((2,))
    pairs_of = pltpu.SemaphoreType.DMA((OWN, 2))
    return pl.pallas_call(
        kernel,
        out_shape=(tile, tile),
        in_specs=[smem] + [vmem] * 10,
        out_specs=(vmem, vmem),
        scratch_shapes=[
            message,
            message,
            halves,
            halves,
            halves,
            halves,
            message,
            message,
            rows,
            rows,
            pltpu.VMEM((HEADS, T, T), F32),
            pltpu.VMEM((HEADS, T, T), F32),
            rows,
            rows,
            pltpu.VMEM((TI, TJ, C), F32),
            pltpu.VMEM((POS, C), F32),
            pltpu.VMEM((POS, C), F32),
            pltpu.VMEM((4, POS, C), F32),
            pltpu.VMEM((POS, C), F32),
            square,
            square,
            square_low,
            square_low,
            square_low,
            square_low,
            square,
            pltpu.VMEM((HEADS, T, T), BF16),
            pltpu.VMEM((HEADS, T, T), BF16),
            rows,
            rows,
            rows,
            rows,
            pltpu.SemaphoreType.REGULAR,
            pair_of,
            pairs_of,
            pairs_of,
            pair_of,
            pair_of,
            pair_of,
            pair_of,
            pairs_of,
            pairs_of,
        ],
        compiler_params=pltpu.CompilerParams(
            collective_id=0, has_side_effects=True, vmem_limit_bytes=48 * 1024 * 1024
        ),
        cost_estimate=pl.CostEstimate(flops=2_000_000_000, bytes_accessed=4_000_000, transcendentals=1_000_000),
    )(
        valid_length,
        pair,
        cotangent,
        tri_bias,
        gain_first.reshape(1, C),
        w_first,
        gain_mid.reshape(1, C),
        w_mid,
        gain_second.reshape(1, C),
        w_second,
        w_att_out,
    )


def solution(mesh):
    return jax.shard_map(
        body,
        mesh=mesh,
        in_specs=(
            P("row", "col", None),
            P("row", "col", None),
            P(None, "col", None),
            P(),
            P(),
            P(),
            P(),
            P(),
            P(),
            P(),
            P(),
        ),
        out_specs=(P("row", "col", None), P("row", "col", None)),
        check_vma=False,
    )
```

```python
import functools
import math

import jax
import jax.numpy as jnp
from jax import lax
from jax.experimental import pallas as pl
from jax.experimental.pallas import tpu as pltpu
from jax.sharding import PartitionSpec as P

EPSILON = 1e-05
MASK_SHIFT = 1000000000.0
MESH = pl.DeviceIdType.MESH
F32 = jnp.float32
BF16 = jnp.bfloat16
NN = (((1,), (0,)), ((), ()))
NT = (((1,), (1,)), ((), ()))

T = 256
C = 128
HEADS = 4
WIDTH = 32
ROWS = 8
COLS = 16
N = ROWS * COLS
TI = T // ROWS
TJ = T // COLS
POS = TI * TJ
OWN = T // N


def split(x):
    hi = x.astype(BF16)
    return hi, (x - hi.astype(F32)).astype(BF16)


def dot(a, b, dims=NN):
    return lax.dot_general(a, b, dims, preferred_element_type=F32)


def mm(a, b, dims=NN):
    return dot(a[0], b[0], dims) + (dot(a[0], b[1], dims) + dot(a[1], b[0], dims))


def norm(u):
    centre = u - jnp.mean(u, axis=0, keepdims=True)
    scale = lax.rsqrt(jnp.mean(centre * centre, axis=0, keepdims=True) + EPSILON)
    return centre * scale, scale


def norm_back(d, xhat, scale):
    mean_d = jnp.mean(d, axis=0, keepdims=True)
    mean_dx = jnp.mean(d * xhat, axis=0, keepdims=True)
    return scale * (d - mean_d - xhat * mean_dx)


def left3(x):
    hi, lo = split(x)
    return jnp.concatenate([hi, lo, hi], axis=1)


def right3(x):
    hi, lo = split(x)
    return jnp.concatenate([hi, hi, lo], axis=0)


def turn(x):
    rows, cols = x.shape
    return jnp.concatenate(
        [
            jnp.concatenate([x[128 * i : 128 * (i + 1), 128 * j : 128 * (j + 1)].T for i in range(rows // 128)], axis=1)
            for j in range(cols // 128)
        ],
        axis=0,
    )


def swap_blocks(xs):
    block = lax.broadcasted_iota(jnp.int32, xs[0].shape, 1) // 32
    for bit in (2, 1):
        upper = (block & bit) != 0
        ys = list(xs)
        for s in range(4):
            if s & bit == 0:
                a, b = xs[s], xs[s | bit]
                ys[s] = jnp.where(upper, pltpu.roll(b, 32 * bit, 1), a)
                ys[s | bit] = jnp.where(upper, b, pltpu.roll(a, 128 - 32 * bit, 1))
        xs = ys
    return xs


def head_keys(x):
    hi = x.astype(BF16).astype(F32)
    again = pltpu.roll(hi, WIDTH, 1)
    lo = pltpu.roll(x - hi, 2 * WIDTH, 1)
    block = lax.broadcasted_iota(jnp.int32, x.shape, 1) // WIDTH
    return [
        jnp.where(block == h, hi, jnp.where(block == (h + 1) % HEADS, again, lo)).astype(BF16) for h in range(HEADS)
    ]


def head_queries(hi, lo, h):
    own = slice(WIDTH * h, WIDTH * (h + 1))
    blocks = [None] * HEADS
    blocks[h] = hi[own]
    blocks[(h + 1) % HEADS] = lo[own]
    blocks[(h + 2) % HEADS] = hi[own]
    blocks[(h + 3) % HEADS] = jnp.zeros_like(hi[own])
    return jnp.concatenate(blocks, axis=0)


def kernel(
    valid_ref,
    pair_any,
    cot_any,
    bias_any,
    gain_first,
    w_first_any,
    gain_mid,
    w_mid_any,
    gain_second,
    w_second_any,
    w_att_out_any,
    out_ref,
    grad_ref,
    send_a,
    recv_a,
    send_x,
    recv_x,
    send_d,
    recv_d,
    send_g,
    recv_g,
    pair_r,
    cot_r,
    bias_r,
    bias_t,
    out_r,
    grad_r,
    grad_t,
    xhat_t,
    scale_t,
    proj_t,
    mask_t,
    at_s,
    bt_s,
    at_hi,
    at_lo,
    bt_hi,
    bt_lo,
    dx_s,
    e_s,
    e_hi,
    e_lo,
    w03_s,
    w4_s,
    w4t_s,
    wm_s,
    wmt_s,
    wo_s,
    wot_s,
    w2_s,
    w2t_s,
    pair_ref,
    w_first,
    w_mid,
    w_second,
    w_att_out,
    sem_in,
    load_sems,
    a_sems,
    x_sems,
    d_sems,
    g_sems,
    pair_sems,
    cot_sems,
    bias_sems,
    twin_sems,
    out_sems,
    grad_sems,
):
    r = lax.axis_index("row")
    c = lax.axis_index("col")
    me = r * COLS + c
    valid = valid_ref[0]

    barrier = pltpu.get_barrier_semaphore()

    def greet_col(i, _):
        pl.semaphore_signal(barrier, inc=1, device_id=(r, lax.rem(c + i, COLS)), device_id_type=MESH)
        return 0

    def greet_row(i, _):
        pl.semaphore_signal(barrier, inc=1, device_id=(lax.rem(r + i, ROWS), c), device_id_type=MESH)
        return 0

    lax.fori_loop(1, COLS, greet_col, 0)
    lax.fori_loop(1, ROWS, greet_row, 0)

    here = pl.ds(pl.multiple_of(c * TJ, TJ), TJ)
    cot_view = cot_any.reshape(OWN, TJ, TJ, C)
    loads = [
        pltpu.make_async_copy(src, dst, load_sems.at[n])
        for n, (src, dst) in enumerate(
            (
                (pair_any, pair_ref),
                (w_first_any, w_first),
                (bias_any, bias_r.at[:, here]),
                (w_second_any, w_second),
                (w_mid_any, w_mid),
                (w_att_out_any, w_att_out),
                (cot_view.at[:, c], cot_r.at[:, here]),
            )
        )
    ]
    for load in loads:
        load.start()

    def send_all(src, dst, sems):
        def go(i, _):
            d = lax.rem(me + i, N)
            pltpu.make_async_remote_copy(
                src(d), dst, sems.at[0], sems.at[1], device_id=(d // COLS, lax.rem(d, COLS)), device_id_type=MESH
            ).start()
            return 0

        lax.fori_loop(1, N, go, 0)

    def send_cols(src, dst, sems):
        def go(i, _):
            d = lax.rem(c + i, COLS)
            pltpu.make_async_remote_copy(
                src(d), dst, sems.at[0], sems.at[1], device_id=(r, d), device_id_type=MESH
            ).start()
            return 0

        lax.fori_loop(1, COLS, go, 0)

    def waiter(view, sems):
        return pltpu.make_async_remote_copy(view, view, sems.at[0], sems.at[1], device_id=(r, c), device_id_type=MESH)

    for load in loads[:2]:
        load.wait()
    pair_flat = pair_ref.reshape(POS, C)
    u = jnp.concatenate(
        [
            jnp.concatenate([pair_flat[pl.ds(4 * q + g, TI, stride=TJ)] for g in range(4)], axis=0).T
            for q in range(4)
        ],
        axis=1,
    )
    xhat, scale = norm(u)
    xhat_t[...] = xhat
    scale_t[...] = jnp.broadcast_to(scale, (8, POS))
    gain = jnp.broadcast_to(gain_first[...], (C, C)).T
    w03 = w_first[:, : 4 * C] * jnp.concatenate([gain] * 4, axis=1)
    w03_s[...] = left3(w03)
    proj = dot(left3(turn(w03)), right3(xhat))
    pos = lax.broadcasted_iota(jnp.int32, (8, POS), 1)
    in_row = (r * TI + pos % TI) < valid
    in_col = (c * TJ + pos // TI) < valid
    mask_t[...] = jnp.where(in_row & in_col, 1.0, 0.0).astype(F32)
    mask = mask_t[0:1]
    sig0 = jax.nn.sigmoid(proj[:C])
    sig2 = jax.nn.sigmoid(proj[2 * C : 3 * C])
    p1 = proj[C : 2 * C]
    p3 = proj[3 * C :]
    proj_t[0] = sig0
    proj_t[1] = p1
    proj_t[2] = sig2
    proj_t[3] = p3
    left = mask * sig0 * p1
    right = mask * sig2 * p3
    sa = send_a.reshape(N * 8, C)
    for q in range(4):
        sa[pl.ds(q, C, stride=8)] = left[:, 128 * q : 128 * (q + 1)]
        sa[pl.ds(4 + q, C, stride=8)] = right[:, 128 * q : 128 * (q + 1)]

    for load in loads[3:6]:
        load.wait()
    w4 = w_first[:, 4 * C :] * gain
    w4_s[...] = left3(w4)
    w4t_s[...] = left3(w4.T)
    w_m = w_mid[...] * jnp.broadcast_to(gain_mid[...], (C, C)).T
    wm_s[...] = left3(w_m)
    wmt_s[...] = left3(w_m.T)
    wo_s[...] = left3(w_att_out[...])
    wot_s[...] = left3(w_att_out[...].T)
    w_sec = w_second[...] * jnp.concatenate([jnp.broadcast_to(gain_second[...], (C, C)).T] * 4, axis=1)
    w2_s[...] = left3(w_sec)
    w2t_s[...] = left3(turn(w_sec))

    pl.semaphore_wait(barrier, COLS - 1 + ROWS - 1)

    def greet_again(i, _):
        pl.semaphore_signal(sem_in, inc=1, device_id=(lax.rem(r + i, ROWS), c), device_id_type=MESH)
        return 0

    lax.fori_loop(1, ROWS, greet_again, 0)
    pl.semaphore_wait(sem_in, ROWS - 1)
    send_all(lambda d: send_a.at[d], recv_a.at[me], a_sems)
    recv_a[me] = send_a[me]

    pair_view = pair_ref.reshape(OWN, TJ, TJ, C)

    def send_bias(i, _):
        d = lax.rem(c + 2 * i, COLS)
        pltpu.make_async_remote_copy(
            bias_any, bias_r.at[:, here], bias_sems.at[0], bias_sems.at[1], device_id=(r, d), device_id_type=MESH
        ).start()
        return 0

    send_cols(lambda d: pair_view.at[:, d], pair_r.at[:, here], pair_sems)
    lax.fori_loop(1, COLS // 2, send_bias, 0)
    pair_r[:, here] = pair_view[:, c]

    waiter(recv_a.at[pl.ds(0, N - 1)], a_sems).wait_recv()
    ra = recv_a.reshape(N * 8, C)
    for part, dest in ((0, at_s), (4, bt_s)):
        for half in range(2):
            for q in range(4):
                ys = swap_blocks(
                    [ra[pl.ds((64 * half + 16 * rr) * 8 + part + q, COLS, stride=8)] for rr in range(4)]
                )
                for g in range(4):
                    dest[pl.ds((4 * q + g) * COLS, COLS), pl.ds(128 * half, 128)] = ys[g]
    at = at_s[...]
    a_parts = split(at.T)
    at_parts = split(at)
    at_hi[...], at_lo[...] = at_parts
    bt_parts = split(bt_s[...])
    bt_hi[...], bt_lo[...] = bt_parts
    x = mm(a_parts, bt_parts)
    sx = send_x.reshape(N * 8, C)
    for l in range(OWN):
        for rr in range(ROWS):
            for jh in range(2):
                sx[pl.ds(16 * rr * 8 + 2 * l + jh, COLS, stride=8)] = x[
                    TI * rr + 16 * l : TI * rr + 16 * (l + 1), 128 * jh : 128 * (jh + 1)
                ]
    send_all(lambda d: send_x.at[d, pl.ds(0, 4)], recv_x.at[me, pl.ds(0, 4)], x_sems)
    recv_x[me] = send_x[me]

    send_cols(lambda d: cot_view.at[:, d], cot_r.at[:, here], cot_sems)
    half_bias = COLS // 2 - 1
    waiter(bias_r.reshape(HEADS * T, T).at[pl.ds(0, HEADS * TJ * half_bias)], bias_sems).wait_recv()
    loads[2].wait()
    odd = lax.rem(c, 2)
    bias_view = bias_r.reshape(HEADS, COLS // 2, 2, TJ, T)
    pltpu.make_async_remote_copy(
        bias_view.at[:, :, odd],
        bias_view.at[:, :, odd],
        twin_sems.at[0],
        twin_sems.at[1],
        device_id=(r, c + 1 - 2 * odd),
        device_id_type=MESH,
    ).start()
    waiter(pair_r.reshape(OWN * T, C).at[pl.ds(0, OWN * TJ * (COLS - 1))], pair_sems).wait_recv()
    pair_t = turn(pair_r.reshape(OWN * T, C)[...])
    ph, ps = norm(pair_t)
    g1 = jax.nn.sigmoid(dot(w4t_s[...], right3(ph)))
    waiter(bias_r.reshape(HEADS * T, T).at[pl.ds(0, HEADS * T // 2)], twin_sems).wait_recv()
    key = lax.broadcasted_iota(jnp.int32, (T, T), 0)
    shift = jnp.where(key < valid, 0.0, -MASK_SHIFT).astype(F32)
    for h in range(HEADS):
        bias_t[h] = bias_r[h].T + shift

    waiter(recv_x.at[pl.ds(0, N - 1), pl.ds(0, 4)], x_sems).wait_recv()
    rx = recv_x.reshape(N * 8, C)
    x = jnp.concatenate([rx[pl.ds(m, C, stride=8)] for m in range(4)], axis=1)
    xh, xs = norm(x)
    m = dot(wmt_s[...], right3(xh))
    z1 = pair_t + g1 * m
    zh, zs = norm(z1)
    second = dot(w2t_s[...], right3(zh))
    score_scale = 1.0 / math.sqrt(WIDTH)
    qt_hi, qt_lo = split(second[:C] * score_scale)
    kt_hi, kt_lo = split(second[C : 2 * C])
    vt_hi, vt_lo = split(second[2 * C : 3 * C])
    g2 = jax.nn.sigmoid(second[3 * C :])
    ots = [[], []]
    inverses = [[], []]
    for l in range(OWN):
        js = slice(T * l, T * (l + 1))
        keys = head_keys(turn(second[C : 2 * C, js]))
        for h in range(HEADS):
            hs = slice(WIDTH * h, WIDTH * (h + 1))
            s = dot(keys[h], head_queries(qt_hi[:, js], qt_lo[:, js], h)) + bias_t[h]
            e = jnp.exp(s - jnp.max(s, axis=0, keepdims=True))
            inverse = 1.0 / jnp.sum(e, axis=0, keepdims=True)
            eh, el = split(e)
            e_s[l, h] = e
            e_hi[l, h] = eh
            e_lo[l, h] = el
            both = dot(jnp.concatenate([vt_hi[hs, js], vt_lo[hs, js]], axis=0), eh)
            ots[l].append((both[:WIDTH] + (both[WIDTH:] + dot(vt_hi[hs, js], el))) * inverse)
            inverses[l].append(inverse)
    o = jnp.concatenate([jnp.concatenate(ots[l], axis=0) for l in range(OWN)], axis=1)

    for load in loads[6:]:
        load.wait()
    waiter(cot_r.reshape(OWN * T, C).at[pl.ds(0, OWN * TJ * (COLS - 1))], cot_sems).wait_recv()
    cot = turn(cot_r.reshape(OWN * T, C)[...])
    dgated = dot(wo_s[...], right3(cot))
    d_o = dgated * g2
    d_s = dgated * o * g2 * (1.0 - g2)
    dqs = [[], []]
    dks = [[], []]
    dvs = [[], []]
    for l in range(OWN):
        js = slice(T * l, T * (l + 1))
        values = head_keys(turn(second[2 * C : 3 * C, js]))
        for h in range(HEADS):
            hs = slice(WIDTH * h, WIDTH * (h + 1))
            part = d_o[hs, js] * inverses[l][h]
            delta = jnp.sum(part * ots[l][h], axis=0, keepdims=True)
            dt_hi, dt_lo = split(part)
            zero = jnp.zeros_like(dt_hi)
            blocks = [None] * HEADS
            for n, block in enumerate((dt_hi, dt_lo, dt_hi, zero)):
                blocks[(h + n) % HEADS] = block
            dp = dot(values[h], jnp.concatenate(blocks, axis=0))
            dsh, dsl = split(e_s[l, h] * (dp - delta))
            both = dot(jnp.concatenate([kt_hi[hs, js], kt_lo[hs, js]], axis=0), dsh)
            dqs[l].append(both[:WIDTH] + (both[WIDTH:] + dot(kt_hi[hs, js], dsl)))
            both = dot(jnp.concatenate([qt_hi[hs, js], qt_lo[hs, js]], axis=0), dsh, NT)
            dks[l].append(both[:WIDTH] + (both[WIDTH:] + dot(qt_hi[hs, js], dsl, NT)))
            both = dot(jnp.concatenate([dt_hi, dt_lo], axis=0), e_hi[l, h], NT)
            dvs[l].append(both[:WIDTH] + (both[WIDTH:] + dot(dt_hi, e_lo[l, h], NT)))

    def stack(parts):
        return jnp.concatenate([jnp.concatenate(parts[l], axis=0) for l in range(OWN)], axis=1)

    d_second = jnp.concatenate([stack(dqs) * score_scale, stack(dks), stack(dvs), d_s], axis=0)
    dz1 = cot + norm_back(dot(w2_s[...], right3(d_second)), zh, zs)
    dx = norm_back(dot(wm_s[...], right3(dz1 * g1)), xh, xs)
    sd = send_d.reshape(N * 8, C)
    for n in range(4):
        sd[pl.ds(n, C, stride=8)] = dx[:, 128 * n : 128 * (n + 1)]
    send_all(lambda d: send_d.at[d, pl.ds(0, 4)], recv_d.at[me, pl.ds(0, 4)], d_sems)
    recv_d[me] = send_d[me]

    out_flat = out_r.reshape(OWN * T, C)
    grad_part = grad_r.reshape(OWN * T, C)
    out_flat[...] = turn(z1 + dot(wot_s[...], right3(g2 * o)))
    for l in range(OWN):
        send_cols(
            lambda d: out_r.at[l, pl.ds(pl.multiple_of(d * TJ, TJ), TJ)], out_ref.at[l * TJ + c], out_sems.at[l]
        )
        out_ref[l * TJ + c] = out_r[l, here]
    dp4 = dz1 * m * g1 * (1.0 - g1)
    grad_part[...] = turn(dz1 + norm_back(dot(w4_s[...], right3(dp4)), ph, ps))
    for l in range(OWN):
        send_cols(
            lambda d: grad_r.at[l, pl.ds(pl.multiple_of(d * TJ, TJ), TJ)], grad_t.at[l * TJ + c], grad_sems.at[l]
        )
        grad_t[l * TJ + c] = grad_r[l, here]

    waiter(recv_d.at[pl.ds(0, N - 1), pl.ds(0, 4)], d_sems).wait_recv()
    rd = recv_d.reshape(N * 8, C)
    for l in range(OWN):
        for rr in range(ROWS):
            for jh in range(2):
                dx_s[pl.ds(TI * rr + 16 * l, 16), pl.ds(128 * jh, 128)] = rd[
                    pl.ds(16 * rr * 8 + 2 * l + jh, COLS, stride=8)
                ]
    dx_parts = split(dx_s[...])
    d_bt = mm((at_hi[...], at_lo[...]), dx_parts)
    d_at = mm((bt_hi[...], bt_lo[...]), dx_parts, NT)
    sg = send_g.reshape(N * 8, C)
    for part, d_src in ((0, d_at), (4, d_bt)):
        for half in range(2):
            for q in range(4):
                ys = swap_blocks(
                    [
                        d_src[(4 * q + g) * COLS : (4 * q + g + 1) * COLS, 128 * half : 128 * (half + 1)]
                        for g in range(4)
                    ]
                )
                for rr in range(4):
                    sg[pl.ds((64 * half + 16 * rr) * 8 + part + q, COLS, stride=8)] = ys[rr]
    send_all(lambda d: send_g.at[d], recv_g.at[me], g_sems)
    recv_g[me] = send_g[me]

    waiter(recv_g.at[pl.ds(0, N - 1)], g_sems).wait_recv()
    rg = recv_g.reshape(N * 8, C)
    mask = mask_t[0:1]
    da = jnp.concatenate([rg[pl.ds(q, C, stride=8)] for q in range(4)], axis=1) * mask
    db = jnp.concatenate([rg[pl.ds(4 + q, C, stride=8)] for q in range(4)], axis=1) * mask
    sig0 = proj_t[0]
    sig2 = proj_t[2]
    dp1 = da * sig0
    dp3 = db * sig2
    dp0 = dp1 * proj_t[1] * (1.0 - sig0)
    dp2 = dp3 * proj_t[3] * (1.0 - sig2)
    du = dot(w03_s[...], right3(jnp.concatenate([dp0, dp1, dp2, dp3], axis=0)))
    res = turn(norm_back(du, xhat_t[...], scale_t[0:1]))
    grad_flat = grad_ref.reshape(POS, C)
    part_flat = grad_t.reshape(POS, C)
    for l in range(OWN):
        waiter(grad_t.at[pl.ds(0, COLS - 1)], grad_sems.at[l]).wait_recv()
    for kk in range(TJ):
        grad_flat[pl.ds(kk, TI, stride=TJ)] = res[TI * kk : TI * (kk + 1)] + part_flat[pl.ds(kk, TI, stride=TJ)]

    waiter(recv_a.at[pl.ds(0, N - 1)], a_sems).wait_send()
    waiter(pair_r.reshape(OWN * T, C).at[pl.ds(0, OWN * TJ * (COLS - 1))], pair_sems).wait_send()
    waiter(cot_r.reshape(OWN * T, C).at[pl.ds(0, OWN * TJ * (COLS - 1))], cot_sems).wait_send()
    waiter(bias_r.reshape(HEADS * T, T).at[pl.ds(0, HEADS * TJ * half_bias)], bias_sems).wait_send()
    waiter(bias_r.reshape(HEADS * T, T).at[pl.ds(0, HEADS * T // 2)], twin_sems).wait_send()
    waiter(recv_g.at[pl.ds(0, N - 1)], g_sems).wait_send()
    waiter(recv_x.at[pl.ds(0, N - 1), pl.ds(0, 4)], x_sems).wait_send()
    waiter(recv_d.at[pl.ds(0, N - 1), pl.ds(0, 4)], d_sems).wait_send()
    for l in range(OWN):
        waiter(grad_t.at[pl.ds(0, COLS - 1)], grad_sems.at[l]).wait_send()
        waiter(out_ref.at[pl.ds(0, COLS - 1)], out_sems.at[l]).wait()


def body(pair, cotangent, tri_bias, valid_length, gain_first, w_first, gain_mid, w_mid, gain_second, w_second, w_att_out):
    vmem = pl.BlockSpec(memory_space=pltpu.VMEM)
    smem = pl.BlockSpec(memory_space=pltpu.SMEM)
    anywhere = pl.BlockSpec(memory_space=pl.ANY)
    tile = jax.ShapeDtypeStruct((TI, TJ, C), F32)
    message = pltpu.VMEM((N, 8, C), F32)
    weight = pltpu.VMEM((C, 3 * C), BF16)
    rows = pltpu.VMEM((OWN, T, C), F32)
    square = pltpu.VMEM((T, T), F32)
    square_low = pltpu.VMEM((T, T), BF16)
    pair_of = pltpu.SemaphoreType.DMA((2,))
    pairs_of = pltpu.SemaphoreType.DMA((OWN, 2))
    return pl.pallas_call(
        kernel,
        out_shape=(tile, tile),
        in_specs=[smem] + [anywhere] * 3 + [vmem, anywhere] * 3 + [anywhere],
        out_specs=(vmem, vmem),
        scratch_shapes=[
            message,
            message,
            message,
            message,
            message,
            message,
            message,
            message,
            rows,
            rows,
            pltpu.VMEM((HEADS, T, T), F32),
            pltpu.VMEM((HEADS, T, T), F32),
            rows,
            rows,
            pltpu.VMEM((TI, TJ, C), F32),
            pltpu.VMEM((C, POS), F32),
            pltpu.VMEM((8, POS), F32),
            pltpu.VMEM((4, C, POS), F32),
            pltpu.VMEM((8, POS), F32),
            square,
            square,
            square_low,
            square_low,
            square_low,
            square_low,
            square,
            pltpu.VMEM((OWN, HEADS, T, T), F32),
            pltpu.VMEM((OWN, HEADS, T, T), BF16),
            pltpu.VMEM((OWN, HEADS, T, T), BF16),
            pltpu.VMEM((C, 12 * C), BF16),
            weight,
            weight,
            weight,
            weight,
            weight,
            weight,
            pltpu.VMEM((C, 12 * C), BF16),
            pltpu.VMEM((4 * C, 3 * C), BF16),
            pltpu.VMEM((TI, TJ, C), F32),
            pltpu.VMEM((C, 5 * C), F32),
            pltpu.VMEM((C, C), F32),
            pltpu.VMEM((C, 4 * C), F32),
            pltpu.VMEM((C, C), F32),
            pltpu.SemaphoreType.REGULAR,
            pltpu.SemaphoreType.DMA((7,)),
            pair_of,
            pair_of,
            pair_of,
            pair_of,
            pair_of,
            pair_of,
            pair_of,
            pair_of,
            pairs_of,
            pairs_of,
        ],
        compiler_params=pltpu.CompilerParams(
            collective_id=0, has_side_effects=True, vmem_limit_bytes=60 * 1024 * 1024
        ),
        cost_estimate=pl.CostEstimate(flops=2_000_000_000, bytes_accessed=4_000_000, transcendentals=1_000_000),
    )(
        valid_length,
        pair,
        cotangent,
        tri_bias,
        gain_first.reshape(1, C),
        w_first,
        gain_mid.reshape(1, C),
        w_mid,
        gain_second.reshape(1, C),
        w_second,
        w_att_out,
    )


def solution(mesh):
    return jax.shard_map(
        body,
        mesh=mesh,
        in_specs=(
            P("row", "col", None),
            P("row", "col", None),
            P(None, "col", None),
            P(),
            P(),
            P(),
            P(),
            P(),
            P(),
            P(),
            P(),
        ),
        out_specs=(P("row", "col", None), P("row", "col", None)),
        check_vma=False,
    )
```

```python
import functools
import math

import jax
import jax.numpy as jnp
from jax import lax
from jax.experimental import pallas as pl
from jax.experimental.pallas import tpu as pltpu
from jax.sharding import PartitionSpec as P

EPSILON = 1e-05
MASK_SHIFT = 1000000000.0
MESH = pl.DeviceIdType.MESH
F32 = jnp.float32
BF16 = jnp.bfloat16
NN = (((1,), (0,)), ((), ()))
NT = (((1,), (1,)), ((), ()))

T = 256
C = 128
HEADS = 4
WIDTH = 32
ROWS = 8
COLS = 16
N = ROWS * COLS
TI = T // ROWS
TJ = T // COLS
POS = TI * TJ
OWN = T // N


def split(x):
    hi = x.astype(BF16)
    return hi, (x - hi.astype(F32)).astype(BF16)


def dot(a, b, dims=NN):
    return lax.dot_general(a, b, dims, preferred_element_type=F32)


def mm(a, b, dims=NN):
    return dot(a[0], b[0], dims) + (dot(a[0], b[1], dims) + dot(a[1], b[0], dims))


def norm(u):
    centre = u - jnp.mean(u, axis=0, keepdims=True)
    scale = lax.rsqrt(jnp.mean(centre * centre, axis=0, keepdims=True) + EPSILON)
    return centre * scale, scale


def norm_back(d, xhat, scale):
    mean_d = jnp.mean(d, axis=0, keepdims=True)
    mean_dx = jnp.mean(d * xhat, axis=0, keepdims=True)
    return scale * (d - mean_d - xhat * mean_dx)


def left3(x):
    hi, lo = split(x)
    return jnp.concatenate([hi, lo, hi], axis=1)


def right3(x):
    hi, lo = split(x)
    return jnp.concatenate([hi, hi, lo], axis=0)


def turn(x):
    rows, cols = x.shape
    return jnp.concatenate(
        [
            jnp.concatenate([x[128 * i : 128 * (i + 1), 128 * j : 128 * (j + 1)].T for i in range(rows // 128)], axis=1)
            for j in range(cols // 128)
        ],
        axis=0,
    )


def swap_blocks(xs):
    block = lax.broadcasted_iota(jnp.int32, xs[0].shape, 1) // 32
    for bit in (2, 1):
        upper = (block & bit) != 0
        ys = list(xs)
        for s in range(4):
            if s & bit == 0:
                a, b = xs[s], xs[s | bit]
                ys[s] = jnp.where(upper, pltpu.roll(b, 32 * bit, 1), a)
                ys[s | bit] = jnp.where(upper, b, pltpu.roll(a, 128 - 32 * bit, 1))
        xs = ys
    return xs


def head_keys(x):
    hi = x.astype(BF16).astype(F32)
    again = pltpu.roll(hi, WIDTH, 1)
    lo = pltpu.roll(x - hi, 2 * WIDTH, 1)
    block = lax.broadcasted_iota(jnp.int32, x.shape, 1) // WIDTH
    return [
        jnp.where(block == h, hi, jnp.where(block == (h + 1) % HEADS, again, lo)).astype(BF16) for h in range(HEADS)
    ]


def head_queries(hi, lo, h):
    own = slice(WIDTH * h, WIDTH * (h + 1))
    blocks = [None] * HEADS
    blocks[h] = hi[own]
    blocks[(h + 1) % HEADS] = lo[own]
    blocks[(h + 2) % HEADS] = hi[own]
    blocks[(h + 3) % HEADS] = jnp.zeros_like(hi[own])
    return jnp.concatenate(blocks, axis=0)


def kernel(
    valid_ref,
    pair_any,
    cot_any,
    bias_any,
    gain_first,
    w_first_any,
    gain_mid,
    w_mid_any,
    gain_second,
    w_second_any,
    w_att_out_any,
    out_ref,
    grad_ref,
    send_a,
    recv_a,
    send_x,
    recv_x,
    send_d,
    recv_d,
    send_g,
    recv_g,
    pair_r,
    cot_r,
    bias_r,
    bias_t,
    out_r,
    grad_r,
    grad_t,
    xhat_t,
    scale_t,
    proj_t,
    mask_t,
    at_s,
    bt_s,
    at_hi,
    at_lo,
    bt_hi,
    bt_lo,
    dx_s,
    e_s,
    e_hi,
    e_lo,
    w03_s,
    w4_s,
    w4t_s,
    wm_s,
    wmt_s,
    wo_s,
    wot_s,
    w2_s,
    w2t_s,
    pair_ref,
    w_first,
    w_mid,
    w_second,
    w_att_out,
    sem_in,
    load_sems,
    a_sems,
    x_sems,
    d_sems,
    g_sems,
    pair_sems,
    cot_sems,
    bias_sems,
    twin_sems,
    out_sems,
    grad_sems,
):
    r = lax.axis_index("row")
    c = lax.axis_index("col")
    me = r * COLS + c
    valid = valid_ref[0]

    barrier = pltpu.get_barrier_semaphore()

    def greet_col(i, _):
        pl.semaphore_signal(barrier, inc=1, device_id=(r, lax.rem(c + i, COLS)), device_id_type=MESH)
        return 0

    def greet_row(i, _):
        pl.semaphore_signal(barrier, inc=1, device_id=(lax.rem(r + i, ROWS), c), device_id_type=MESH)
        return 0

    lax.fori_loop(1, COLS, greet_col, 0)
    lax.fori_loop(1, ROWS, greet_row, 0)

    here = pl.ds(pl.multiple_of(c * TJ, TJ), TJ)
    cot_view = cot_any.reshape(OWN, TJ, TJ, C)
    loads = [
        pltpu.make_async_copy(src, dst, load_sems.at[n])
        for n, (src, dst) in enumerate(
            (
                (pair_any, pair_ref),
                (w_first_any, w_first),
                (bias_any, bias_r.at[:, here]),
                (w_second_any, w_second),
                (w_mid_any, w_mid),
                (w_att_out_any, w_att_out),
                (cot_view.at[:, c], cot_r.at[:, here]),
            )
        )
    ]
    for load in loads:
        load.start()

    def send_all(src, dst, sems):
        def go(i, _):
            d = lax.rem(me + i, N)
            pltpu.make_async_remote_copy(
                src(d), dst, sems.at[0], sems.at[1], device_id=(d // COLS, lax.rem(d, COLS)), device_id_type=MESH
            ).start()
            return 0

        lax.fori_loop(1, N, go, 0)

    def send_cols(src, dst, sems):
        def go(i, _):
            d = lax.rem(c + i, COLS)
            pltpu.make_async_remote_copy(
                src(d), dst, sems.at[0], sems.at[1], device_id=(r, d), device_id_type=MESH
            ).start()
            return 0

        lax.fori_loop(1, COLS, go, 0)

    def waiter(view, sems):
        return pltpu.make_async_remote_copy(view, view, sems.at[0], sems.at[1], device_id=(r, c), device_id_type=MESH)

    for load in loads[:2]:
        load.wait()
    pair_flat = pair_ref.reshape(POS, C)
    u = jnp.concatenate(
        [
            jnp.concatenate([pair_flat[pl.ds(4 * q + g, TI, stride=TJ)] for g in range(4)], axis=0).T
            for q in range(4)
        ],
        axis=1,
    )
    xhat, scale = norm(u)
    xhat_t[...] = xhat
    scale_t[...] = jnp.broadcast_to(scale, (8, POS))
    gain = jnp.broadcast_to(gain_first[...], (C, C)).T
    w03 = w_first[:, : 4 * C] * jnp.concatenate([gain] * 4, axis=1)
    w03_s[...] = left3(w03)
    proj = dot(left3(turn(w03)), right3(xhat))
    pos = lax.broadcasted_iota(jnp.int32, (8, POS), 1)
    in_row = (r * TI + pos % TI) < valid
    in_col = (c * TJ + pos // TI) < valid
    mask_t[...] = jnp.where(in_row & in_col, 1.0, 0.0).astype(F32)
    mask = mask_t[0:1]
    sig0 = jax.nn.sigmoid(proj[:C])
    sig2 = jax.nn.sigmoid(proj[2 * C : 3 * C])
    p1 = proj[C : 2 * C]
    p3 = proj[3 * C :]
    proj_t[0] = sig0
    proj_t[1] = p1
    proj_t[2] = sig2
    proj_t[3] = p3
    left = mask * sig0 * p1
    right = mask * sig2 * p3
    sa = send_a.reshape(N * 8, C)
    for q in range(4):
        sa[pl.ds(q, C, stride=8)] = left[:, 128 * q : 128 * (q + 1)]
        sa[pl.ds(4 + q, C, stride=8)] = right[:, 128 * q : 128 * (q + 1)]

    for load in loads[3:6]:
        load.wait()
    w4 = w_first[:, 4 * C :] * gain
    w4_s[...] = left3(w4)
    w4t_s[...] = left3(w4.T)
    w_m = w_mid[...] * jnp.broadcast_to(gain_mid[...], (C, C)).T
    wm_s[...] = left3(w_m)
    wmt_s[...] = left3(w_m.T)
    wo_s[...] = left3(w_att_out[...])
    wot_s[...] = left3(w_att_out[...].T)
    w_sec = w_second[...] * jnp.concatenate([jnp.broadcast_to(gain_second[...], (C, C)).T] * 4, axis=1)
    w2_s[...] = left3(w_sec)
    w2t_s[...] = left3(turn(w_sec))

    pl.semaphore_wait(barrier, COLS - 1 + ROWS - 1)

    def greet_again(i, _):
        pl.semaphore_signal(sem_in, inc=1, device_id=(lax.rem(r + i, ROWS), c), device_id_type=MESH)
        return 0

    lax.fori_loop(1, ROWS, greet_again, 0)
    pl.semaphore_wait(sem_in, ROWS - 1)
    send_all(lambda d: send_a.at[d], recv_a.at[me], a_sems)
    recv_a[me] = send_a[me]

    pair_view = pair_ref.reshape(OWN, TJ, TJ, C)

    def send_bias(i, _):
        d = lax.rem(c + 2 * i, COLS)
        pltpu.make_async_remote_copy(
            bias_any, bias_r.at[:, here], bias_sems.at[0], bias_sems.at[1], device_id=(r, d), device_id_type=MESH
        ).start()
        return 0

    lax.fori_loop(1, COLS // 2, send_bias, 0)
    send_cols(lambda d: pair_view.at[:, d], pair_r.at[:, here], pair_sems)
    pair_r[:, here] = pair_view[:, c]

    waiter(recv_a.at[pl.ds(0, N - 1)], a_sems).wait_recv()
    ra = recv_a.reshape(N * 8, C)
    for part, dest in ((0, at_s), (4, bt_s)):
        for half in range(2):
            for q in range(4):
                ys = swap_blocks(
                    [ra[pl.ds((64 * half + 16 * rr) * 8 + part + q, COLS, stride=8)] for rr in range(4)]
                )
                for g in range(4):
                    dest[pl.ds((4 * q + g) * COLS, COLS), pl.ds(128 * half, 128)] = ys[g]
    at = at_s[...]
    a_parts = split(at.T)
    at_parts = split(at)
    at_hi[...], at_lo[...] = at_parts
    bt_parts = split(bt_s[...])
    bt_hi[...], bt_lo[...] = bt_parts
    x = mm(a_parts, bt_parts)
    sx = send_x.reshape(N * 8, C)
    for l in range(OWN):
        for rr in range(ROWS):
            for jh in range(2):
                sx[pl.ds(16 * rr * 8 + 2 * l + jh, COLS, stride=8)] = x[
                    TI * rr + 16 * l : TI * rr + 16 * (l + 1), 128 * jh : 128 * (jh + 1)
                ]
    send_all(lambda d: send_x.at[d, pl.ds(0, 4)], recv_x.at[me, pl.ds(0, 4)], x_sems)
    recv_x[me] = send_x[me]

    send_cols(lambda d: cot_view.at[:, d], cot_r.at[:, here], cot_sems)
    half_bias = COLS // 2 - 1
    waiter(bias_r.reshape(HEADS * T, T).at[pl.ds(0, HEADS * TJ * half_bias)], bias_sems).wait_recv()
    loads[2].wait()
    odd = lax.rem(c, 2)
    bias_view = bias_r.reshape(HEADS, COLS // 2, 2, TJ, T)
    pltpu.make_async_remote_copy(
        bias_view.at[:, :, odd],
        bias_view.at[:, :, odd],
        twin_sems.at[0],
        twin_sems.at[1],
        device_id=(r, c + 1 - 2 * odd),
        device_id_type=MESH,
    ).start()
    waiter(pair_r.reshape(OWN * T, C).at[pl.ds(0, OWN * TJ * (COLS - 1))], pair_sems).wait_recv()
    pair_t = turn(pair_r.reshape(OWN * T, C)[...])
    ph, ps = norm(pair_t)
    g1 = jax.nn.sigmoid(dot(w4t_s[...], right3(ph)))
    waiter(bias_r.reshape(HEADS * T, T).at[pl.ds(0, HEADS * T // 2)], twin_sems).wait_recv()
    key = lax.broadcasted_iota(jnp.int32, (T, T), 0)
    shift = jnp.where(key < valid, 0.0, -MASK_SHIFT).astype(F32)
    for h in range(HEADS):
        bias_t[h] = bias_r[h].T + shift

    waiter(recv_x.at[pl.ds(0, N - 1), pl.ds(0, 4)], x_sems).wait_recv()
    rx = recv_x.reshape(N * 8, C)
    x = jnp.concatenate([rx[pl.ds(m, C, stride=8)] for m in range(4)], axis=1)
    xh, xs = norm(x)
    m = dot(wmt_s[...], right3(xh))
    z1 = pair_t + g1 * m
    zh, zs = norm(z1)
    second = dot(w2t_s[...], right3(zh))
    score_scale = 1.0 / math.sqrt(WIDTH)
    qt_hi, qt_lo = split(second[:C] * score_scale)
    kt_hi, kt_lo = split(second[C : 2 * C])
    vt_hi, vt_lo = split(second[2 * C : 3 * C])
    g2 = jax.nn.sigmoid(second[3 * C :])
    ots = [[], []]
    inverses = [[], []]
    for l in range(OWN):
        js = slice(T * l, T * (l + 1))
        keys = head_keys(turn(second[C : 2 * C, js]))
        for h in range(HEADS):
            hs = slice(WIDTH * h, WIDTH * (h + 1))
            s = dot(keys[h], head_queries(qt_hi[:, js], qt_lo[:, js], h)) + bias_t[h]
            e = jnp.exp(s - jnp.max(s, axis=0, keepdims=True))
            inverse = 1.0 / jnp.sum(e, axis=0, keepdims=True)
            eh, el = split(e)
            e_s[l, h] = e
            e_hi[l, h] = eh
            e_lo[l, h] = el
            both = dot(jnp.concatenate([vt_hi[hs, js], vt_lo[hs, js]], axis=0), eh)
            ots[l].append((both[:WIDTH] + (both[WIDTH:] + dot(vt_hi[hs, js], el))) * inverse)
            inverses[l].append(inverse)
    o = jnp.concatenate([jnp.concatenate(ots[l], axis=0) for l in range(OWN)], axis=1)

    out_flat = out_r.reshape(OWN * T, C)
    out_flat[...] = turn(z1 + dot(wot_s[...], right3(g2 * o)))
    for l in range(OWN):
        send_cols(
            lambda d: out_r.at[l, pl.ds(pl.multiple_of(d * TJ, TJ), TJ)], out_ref.at[l * TJ + c], out_sems.at[l]
        )
        out_ref[l * TJ + c] = out_r[l, here]

    for load in loads[6:]:
        load.wait()
    waiter(cot_r.reshape(OWN * T, C).at[pl.ds(0, OWN * TJ * (COLS - 1))], cot_sems).wait_recv()
    cot = turn(cot_r.reshape(OWN * T, C)[...])
    dgated = dot(wo_s[...], right3(cot))
    d_o = dgated * g2
    d_s = dgated * o * g2 * (1.0 - g2)
    dqs = [[], []]
    dks = [[], []]
    dvs = [[], []]
    for l in range(OWN):
        js = slice(T * l, T * (l + 1))
        values = head_keys(turn(second[2 * C : 3 * C, js]))
        for h in range(HEADS):
            hs = slice(WIDTH * h, WIDTH * (h + 1))
            part = d_o[hs, js] * inverses[l][h]
            delta = jnp.sum(part * ots[l][h], axis=0, keepdims=True)
            dt_hi, dt_lo = split(part)
            zero = jnp.zeros_like(dt_hi)
            blocks = [None] * HEADS
            for n, block in enumerate((dt_hi, dt_lo, dt_hi, zero)):
                blocks[(h + n) % HEADS] = block
            dp = dot(values[h], jnp.concatenate(blocks, axis=0))
            dsh, dsl = split(e_s[l, h] * (dp - delta))
            both = dot(jnp.concatenate([kt_hi[hs, js], kt_lo[hs, js]], axis=0), dsh)
            dqs[l].append(both[:WIDTH] + (both[WIDTH:] + dot(kt_hi[hs, js], dsl)))
            both = dot(jnp.concatenate([qt_hi[hs, js], qt_lo[hs, js]], axis=0), dsh, NT)
            dks[l].append(both[:WIDTH] + (both[WIDTH:] + dot(qt_hi[hs, js], dsl, NT)))
            both = dot(jnp.concatenate([dt_hi, dt_lo], axis=0), e_hi[l, h], NT)
            dvs[l].append(both[:WIDTH] + (both[WIDTH:] + dot(dt_hi, e_lo[l, h], NT)))

    def stack(parts):
        return jnp.concatenate([jnp.concatenate(parts[l], axis=0) for l in range(OWN)], axis=1)

    d_second = jnp.concatenate([stack(dqs) * score_scale, stack(dks), stack(dvs), d_s], axis=0)
    dz1 = cot + norm_back(dot(w2_s[...], right3(d_second)), zh, zs)
    dx = norm_back(dot(wm_s[...], right3(dz1 * g1)), xh, xs)
    sd = send_d.reshape(N * 8, C)
    for n in range(4):
        sd[pl.ds(n, C, stride=8)] = dx[:, 128 * n : 128 * (n + 1)]
    send_all(lambda d: send_d.at[d, pl.ds(0, 4)], recv_d.at[me, pl.ds(0, 4)], d_sems)
    recv_d[me] = send_d[me]

    grad_part = grad_r.reshape(OWN * T, C)
    dp4 = dz1 * m * g1 * (1.0 - g1)
    grad_part[...] = turn(dz1 + norm_back(dot(w4_s[...], right3(dp4)), ph, ps))
    for l in range(OWN):
        send_cols(
            lambda d: grad_r.at[l, pl.ds(pl.multiple_of(d * TJ, TJ), TJ)], grad_t.at[l * TJ + c], grad_sems.at[l]
        )
        grad_t[l * TJ + c] = grad_r[l, here]

    waiter(recv_d.at[pl.ds(0, N - 1), pl.ds(0, 4)], d_sems).wait_recv()
    rd = recv_d.reshape(N * 8, C)
    for l in range(OWN):
        for rr in range(ROWS):
            for jh in range(2):
                dx_s[pl.ds(TI * rr + 16 * l, 16), pl.ds(128 * jh, 128)] = rd[
                    pl.ds(16 * rr * 8 + 2 * l + jh, COLS, stride=8)
                ]
    dx_parts = split(dx_s[...])
    d_bt = mm((at_hi[...], at_lo[...]), dx_parts)
    d_at = mm((bt_hi[...], bt_lo[...]), dx_parts, NT)
    sg = send_g.reshape(N * 8, C)
    for part, d_src in ((0, d_at), (4, d_bt)):
        for half in range(2):
            for q in range(4):
                ys = swap_blocks(
                    [
                        d_src[(4 * q + g) * COLS : (4 * q + g + 1) * COLS, 128 * half : 128 * (half + 1)]
                        for g in range(4)
                    ]
                )
                for rr in range(4):
                    sg[pl.ds((64 * half + 16 * rr) * 8 + part + q, COLS, stride=8)] = ys[rr]
    send_all(lambda d: send_g.at[d], recv_g.at[me], g_sems)
    recv_g[me] = send_g[me]

    waiter(recv_g.at[pl.ds(0, N - 1)], g_sems).wait_recv()
    rg = recv_g.reshape(N * 8, C)
    mask = mask_t[0:1]
    da = jnp.concatenate([rg[pl.ds(q, C, stride=8)] for q in range(4)], axis=1) * mask
    db = jnp.concatenate([rg[pl.ds(4 + q, C, stride=8)] for q in range(4)], axis=1) * mask
    sig0 = proj_t[0]
    sig2 = proj_t[2]
    dp1 = da * sig0
    dp3 = db * sig2
    dp0 = dp1 * proj_t[1] * (1.0 - sig0)
    dp2 = dp3 * proj_t[3] * (1.0 - sig2)
    du = dot(w03_s[...], right3(jnp.concatenate([dp0, dp1, dp2, dp3], axis=0)))
    res = turn(norm_back(du, xhat_t[...], scale_t[0:1]))
    grad_flat = grad_ref.reshape(POS, C)
    part_flat = grad_t.reshape(POS, C)
    for l in range(OWN):
        waiter(grad_t.at[pl.ds(0, COLS - 1)], grad_sems.at[l]).wait_recv()
    for kk in range(TJ):
        grad_flat[pl.ds(kk, TI, stride=TJ)] = res[TI * kk : TI * (kk + 1)] + part_flat[pl.ds(kk, TI, stride=TJ)]

    waiter(recv_a.at[pl.ds(0, N - 1)], a_sems).wait_send()
    waiter(pair_r.reshape(OWN * T, C).at[pl.ds(0, OWN * TJ * (COLS - 1))], pair_sems).wait_send()
    waiter(cot_r.reshape(OWN * T, C).at[pl.ds(0, OWN * TJ * (COLS - 1))], cot_sems).wait_send()
    waiter(bias_r.reshape(HEADS * T, T).at[pl.ds(0, HEADS * TJ * half_bias)], bias_sems).wait_send()
    waiter(bias_r.reshape(HEADS * T, T).at[pl.ds(0, HEADS * T // 2)], twin_sems).wait_send()
    waiter(recv_g.at[pl.ds(0, N - 1)], g_sems).wait_send()
    waiter(recv_x.at[pl.ds(0, N - 1), pl.ds(0, 4)], x_sems).wait_send()
    waiter(recv_d.at[pl.ds(0, N - 1), pl.ds(0, 4)], d_sems).wait_send()
    for l in range(OWN):
        waiter(grad_t.at[pl.ds(0, COLS - 1)], grad_sems.at[l]).wait_send()
        waiter(out_ref.at[pl.ds(0, COLS - 1)], out_sems.at[l]).wait()


def body(pair, cotangent, tri_bias, valid_length, gain_first, w_first, gain_mid, w_mid, gain_second, w_second, w_att_out):
    vmem = pl.BlockSpec(memory_space=pltpu.VMEM)
    smem = pl.BlockSpec(memory_space=pltpu.SMEM)
    anywhere = pl.BlockSpec(memory_space=pl.ANY)
    tile = jax.ShapeDtypeStruct((TI, TJ, C), F32)
    message = pltpu.VMEM((N, 8, C), F32)
    weight = pltpu.VMEM((C, 3 * C), BF16)
    rows = pltpu.VMEM((OWN, T, C), F32)
    square = pltpu.VMEM((T, T), F32)
    square_low = pltpu.VMEM((T, T), BF16)
    pair_of = pltpu.SemaphoreType.DMA((2,))
    pairs_of = pltpu.SemaphoreType.DMA((OWN, 2))
    return pl.pallas_call(
        kernel,
        out_shape=(tile, tile),
        in_specs=[smem] + [anywhere] * 3 + [vmem, anywhere] * 3 + [anywhere],
        out_specs=(vmem, vmem),
        scratch_shapes=[
            message,
            message,
            message,
            message,
            message,
            message,
            message,
            message,
            rows,
            rows,
            pltpu.VMEM((HEADS, T, T), F32),
            pltpu.VMEM((HEADS, T, T), F32),
            rows,
            rows,
            pltpu.VMEM((TI, TJ, C), F32),
            pltpu.VMEM((C, POS), F32),
            pltpu.VMEM((8, POS), F32),
            pltpu.VMEM((4, C, POS), F32),
            pltpu.VMEM((8, POS), F32),
            square,
            square,
            square_low,
            square_low,
            square_low,
            square_low,
            square,
            pltpu.VMEM((OWN, HEADS, T, T), F32),
            pltpu.VMEM((OWN, HEADS, T, T), BF16),
            pltpu.VMEM((OWN, HEADS, T, T), BF16),
            pltpu.VMEM((C, 12 * C), BF16),
            weight,
            weight,
            weight,
            weight,
            weight,
            weight,
            pltpu.VMEM((C, 12 * C), BF16),
            pltpu.VMEM((4 * C, 3 * C), BF16),
            pltpu.VMEM((TI, TJ, C), F32),
            pltpu.VMEM((C, 5 * C), F32),
            pltpu.VMEM((C, C), F32),
            pltpu.VMEM((C, 4 * C), F32),
            pltpu.VMEM((C, C), F32),
            pltpu.SemaphoreType.REGULAR,
            pltpu.SemaphoreType.DMA((7,)),
            pair_of,
            pair_of,
            pair_of,
            pair_of,
            pair_of,
            pair_of,
            pair_of,
            pair_of,
            pairs_of,
            pairs_of,
        ],
        compiler_params=pltpu.CompilerParams(
            collective_id=0, has_side_effects=True, vmem_limit_bytes=60 * 1024 * 1024
        ),
        cost_estimate=pl.CostEstimate(flops=2_000_000_000, bytes_accessed=4_000_000, transcendentals=1_000_000),
    )(
        valid_length,
        pair,
        cotangent,
        tri_bias,
        gain_first.reshape(1, C),
        w_first,
        gain_mid.reshape(1, C),
        w_mid,
        gain_second.reshape(1, C),
        w_second,
        w_att_out,
    )


def solution(mesh):
    return jax.shard_map(
        body,
        mesh=mesh,
        in_specs=(
            P("row", "col", None),
            P("row", "col", None),
            P(None, "col", None),
            P(),
            P(),
            P(),
            P(),
            P(),
            P(),
            P(),
            P(),
        ),
        out_specs=(P("row", "col", None), P("row", "col", None)),
        check_vma=False,
    )
```

```python
import itertools
import math

import jax
import jax.numpy as jnp
from jax import lax
from jax.experimental import pallas as pl
from jax.experimental.pallas import tpu as pltpu
from jax.sharding import PartitionSpec as P

EPSILON = 1e-05
MASK_SHIFT = 1000000000.0
MESH = pl.DeviceIdType.MESH
F32 = jnp.float32
BF16 = jnp.bfloat16
NN = (((1,), (0,)), ((), ()))
NT = (((1,), (1,)), ((), ()))

T = 256
C = 128
HEADS = 4
WIDTH = 32
ROWS = 8
COLS = 16
N = ROWS * COLS
TI = T // ROWS
TJ = T // COLS
POS = TI * TJ
OWN = T // N


def split(x):
    hi = x.astype(BF16)
    return hi, (x - hi.astype(F32)).astype(BF16)


def dot(a, b, dims=NN):
    return lax.dot_general(a, b, dims, preferred_element_type=F32)


def mm(a, b, dims=NN):
    return dot(a[0], b[0], dims) + (dot(a[0], b[1], dims) + dot(a[1], b[0], dims))


def norm(u):
    centre = u - jnp.mean(u, axis=0, keepdims=True)
    scale = lax.rsqrt(jnp.mean(centre * centre, axis=0, keepdims=True) + EPSILON)
    return centre * scale, scale


def norm_back(d, xhat, scale):
    mean_d = jnp.mean(d, axis=0, keepdims=True)
    mean_dx = jnp.mean(d * xhat, axis=0, keepdims=True)
    return scale * (d - mean_d - xhat * mean_dx)


def left3(x):
    hi, lo = split(x)
    return jnp.concatenate([hi, lo, hi], axis=1)


def right3(x):
    hi, lo = split(x)
    return jnp.concatenate([hi, hi, lo], axis=0)


def turn(x):
    rows, cols = x.shape
    return jnp.concatenate(
        [
            jnp.concatenate([x[128 * i : 128 * (i + 1), 128 * j : 128 * (j + 1)].T for i in range(rows // 128)], axis=1)
            for j in range(cols // 128)
        ],
        axis=0,
    )


def swap_blocks(xs):
    block = lax.broadcasted_iota(jnp.int32, xs[0].shape, 1) // 32
    for bit in (2, 1):
        upper = (block & bit) != 0
        ys = list(xs)
        for s in range(4):
            if s & bit == 0:
                a, b = xs[s], xs[s | bit]
                ys[s] = jnp.where(upper, pltpu.roll(b, 32 * bit, 1), a)
                ys[s | bit] = jnp.where(upper, b, pltpu.roll(a, 128 - 32 * bit, 1))
        xs = ys
    return xs


def head_keys(x):
    hi = x.astype(BF16).astype(F32)
    again = pltpu.roll(hi, WIDTH, 1)
    lo = pltpu.roll(x - hi, 2 * WIDTH, 1)
    block = lax.broadcasted_iota(jnp.int32, x.shape, 1) // WIDTH
    return [
        jnp.where(block == h, hi, jnp.where(block == (h + 1) % HEADS, again, lo)).astype(BF16) for h in range(HEADS)
    ]


def head_queries(hi, lo, h):
    own = slice(WIDTH * h, WIDTH * (h + 1))
    blocks = [None] * HEADS
    blocks[h] = hi[own]
    blocks[(h + 1) % HEADS] = lo[own]
    blocks[(h + 2) % HEADS] = hi[own]
    blocks[(h + 3) % HEADS] = jnp.zeros_like(hi[own])
    return jnp.concatenate(blocks, axis=0)


def kernel(
    valid_ref,
    pair_any,
    cot_any,
    bias_any,
    gain_first_any,
    w_first_any,
    gain_mid_any,
    w_mid_any,
    gain_second_any,
    w_second_any,
    w_att_out_any,
    out_ref,
    grad_ref,
    send_a,
    recv_a,
    send_b,
    recv_b,
    send_x,
    recv_x,
    send_d,
    recv_d,
    send_ga,
    recv_ga,
    send_gb,
    recv_gb,
    pair_r,
    cot_r,
    bias_r,
    bias_t,
    out_r,
    grad_r,
    grad_t,
    xhat_t,
    scale_t,
    proj_t,
    mask_t,
    at_s,
    bt_s,
    at_hi,
    at_lo,
    bt_hi,
    bt_lo,
    dx_s,
    e_s,
    e_hi,
    e_lo,
    w03_s,
    w4_s,
    w4t_s,
    wm_s,
    wmt_s,
    wo_s,
    wot_s,
    w2_s,
    w2t_s,
    pair_ref,
    w_first,
    w_mid,
    w_second,
    w_att_out,
    gain_first,
    gain_mid,
    gain_second,
    sem_in,
    load_sems,
    a_sems,
    b_sems,
    x_sems,
    d_sems,
    ga_sems,
    gb_sems,
    pair_sems,
    cot_sems,
    bias_sems,
    twin_sems,
    out_sems,
    grad_sems,
):
    r = lax.axis_index("row")
    c = lax.axis_index("col")
    me = r * COLS + c
    valid = valid_ref[0]

    barrier = pltpu.get_barrier_semaphore()

    def column(t):
        near = lax.div(t, 8)
        step = lax.div(lax.rem(t, 8), 2)
        z = lax.rem(lax.div(c, 4) + 2 + 3 * step + 3 * lax.div(step * (step - 1), 2), 4)
        hi = lax.rem(lax.div(c, 2) + 1 - near, 2)
        core = lax.rem(c + 1 - lax.rem(t, 2), 2)
        return 4 * z + 2 * hi + core

    def greet_col(t, _):
        pl.semaphore_signal(barrier, inc=1, device_id=(r, column(t)), device_id_type=MESH)
        return 0

    def greet_row(i, _):
        pl.semaphore_signal(barrier, inc=1, device_id=(lax.rem(r + i, ROWS), c), device_id_type=MESH)
        return 0


    here = pl.ds(pl.multiple_of(c * TJ, TJ), TJ)
    cot_view = cot_any.reshape(OWN, TJ, TJ, C)
    loads = [
        pltpu.make_async_copy(src, dst, load_sems.at[n])
        for n, (src, dst) in enumerate(
            (
                (pair_any, pair_ref),
                (w_first_any, w_first),
                (gain_first_any, gain_first),
                (gain_mid_any, gain_mid),
                (gain_second_any, gain_second),
                (bias_any, bias_r.at[:, here]),
                (w_second_any, w_second),
                (w_mid_any, w_mid),
                (w_att_out_any, w_att_out),
                (cot_view.at[:, c], cot_r.at[:, here]),
            )
        )
    ]
    for load in loads:
        load.start()

    x_at = lax.rem(lax.div(c, 2), 2) * 2 + lax.div(r, 4)
    xs_at = [lax.rem(x_at + n, 4) for n in range(4)]
    row_of_x = [4 * lax.rem(v, 2) for v in xs_at]
    col_of_x = [2 * lax.div(v, 2) for v in xs_at]
    row_of_y = [lax.rem(lax.rem(r, 4) + n, 4) for n in range(4)]
    col_of_z = [4 * lax.rem(lax.div(c, 4) + n, 4) for n in range(4)]

    def for_all(visit):
        for hops in sorted(itertools.product(range(3), repeat=3), key=lambda h: -sum(h)):
            ones = [axis for axis in range(3) if hops[axis] == 1]

            def go(t, _):
                def pick(options, axis):
                    if axis not in ones:
                        return options[hops[axis]]
                    sign = lax.rem(lax.div(t, 2 ** (1 + ones.index(axis))), 2)
                    return options[1] + sign * (options[3] - options[1])

                row = pick(row_of_x, 0) + pick(row_of_y, 1)
                core = lax.rem(c + lax.rem(t, 2), 2)
                col = pick(col_of_x, 0) + pick(col_of_z, 2) + core
                visit(row, col)
                return 0

            lax.fori_loop(0 if sum(hops) else 1, 2 ** (1 + len(ones)), go, 0, unroll=True)

    def send_all(src, dst, sems):
        def visit(row, col):
            pltpu.make_async_remote_copy(
                src(row * COLS + col), dst, sems.at[0], sems.at[1], device_id=(row, col), device_id_type=MESH
            ).start()

        for_all(visit)

    def greet(row, col):
        pl.semaphore_signal(barrier, inc=1, device_id=(row, col), device_id_type=MESH)

    for_all(greet)

    def send_cols(src, dst, sems):
        def go(t, _):
            d = column(t)
            pltpu.make_async_remote_copy(
                src(d), dst, sems.at[0], sems.at[1], device_id=(r, d), device_id_type=MESH
            ).start()
            return 0

        lax.fori_loop(0, COLS - 1, go, 0)

    def waiter(view, sems):
        return pltpu.make_async_remote_copy(view, view, sems.at[0], sems.at[1], device_id=(r, c), device_id_type=MESH)

    for load in loads[:3]:
        load.wait()
    pair_flat = pair_ref.reshape(POS, C)
    u = jnp.concatenate(
        [
            jnp.concatenate([pair_flat[pl.ds(4 * q + g, TI, stride=TJ)] for g in range(4)], axis=0).T
            for q in range(4)
        ],
        axis=1,
    )
    xhat, scale = norm(u)
    xhat_t[...] = xhat
    scale_t[...] = jnp.broadcast_to(scale, (8, POS))
    gain = jnp.broadcast_to(gain_first[...], (C, C)).T
    w03 = w_first[:, : 4 * C] * jnp.concatenate([gain] * 4, axis=1)
    w03_s[0] = left3(w03[:, : 2 * C])
    w03_s[1] = left3(w03[:, 2 * C :])
    proj = dot(left3(turn(w03)), right3(xhat))
    pos = lax.broadcasted_iota(jnp.int32, (8, POS), 1)
    in_row = (r * TI + pos % TI) < valid
    in_col = (c * TJ + pos // TI) < valid
    mask_t[...] = jnp.where(in_row & in_col, 1.0, 0.0).astype(F32)
    mask = mask_t[0:1]
    sig0 = jax.nn.sigmoid(proj[:C])
    sig2 = jax.nn.sigmoid(proj[2 * C : 3 * C])
    p1 = proj[C : 2 * C]
    p3 = proj[3 * C :]
    proj_t[0] = sig0
    proj_t[1] = p1
    proj_t[2] = sig2
    proj_t[3] = p3
    left = mask * sig0 * p1
    right = mask * sig2 * p3
    sa = send_a.reshape(N * 8, C)
    sb = send_b.reshape(N * 8, C)
    for q in range(4):
        sa[pl.ds(q, C, stride=8)] = left[:, 128 * q : 128 * (q + 1)]
        sb[pl.ds(q, C, stride=8)] = right[:, 128 * q : 128 * (q + 1)]


    def greet_again(i, _):
        pl.semaphore_signal(sem_in, inc=1, device_id=(lax.rem(r + i, ROWS), c), device_id_type=MESH)
        return 0

    pl.semaphore_wait(barrier, N - 1)
    send_all(lambda d: send_b.at[d, pl.ds(0, 4)], recv_b.at[me, pl.ds(0, 4)], b_sems)
    recv_b[me] = send_b[me]
    send_all(lambda d: send_a.at[d, pl.ds(0, 4)], recv_a.at[me, pl.ds(0, 4)], a_sems)
    recv_a[me] = send_a[me]

    pair_view = pair_ref.reshape(OWN, TJ, TJ, C)

    def send_bias(i, _):
        d = column(2 * i + 1)
        pltpu.make_async_remote_copy(
            bias_any, bias_r.at[:, here], bias_sems.at[0], bias_sems.at[1], device_id=(r, d), device_id_type=MESH
        ).start()
        return 0

    lax.fori_loop(0, COLS // 2 - 1, send_bias, 0)
    send_cols(lambda d: pair_view.at[:, d], pair_r.at[:, here], pair_sems)
    pair_r[:, here] = pair_view[:, c]

    for load in loads[3:5] + loads[6:9]:
        load.wait()
    w4 = w_first[:, 4 * C :] * gain
    w4_s[...] = left3(w4)
    w4t_s[...] = left3(w4.T)
    w_m = w_mid[...] * jnp.broadcast_to(gain_mid[...], (C, C)).T
    wm_s[...] = left3(w_m)
    wmt_s[...] = left3(w_m.T)
    wo_s[...] = left3(w_att_out[...])
    wot_s[...] = left3(w_att_out[...].T)
    w_sec = w_second[...] * jnp.concatenate([jnp.broadcast_to(gain_second[...], (C, C)).T] * 4, axis=1)
    w2_s[...] = left3(w_sec)
    w2t_s[...] = left3(turn(w_sec))

    def factor(landing, sems, dest):
        waiter(landing.at[pl.ds(0, N - 1), pl.ds(0, 4)], sems).wait_recv()
        ra = landing.reshape(N * 8, C)
        for half in range(2):
            for q in range(4):
                ys = swap_blocks([ra[pl.ds((64 * half + 16 * rr) * 8 + q, COLS, stride=8)] for rr in range(4)])
                for g in range(4):
                    dest[pl.ds((4 * q + g) * COLS, COLS), pl.ds(128 * half, 128)] = ys[g]
        return dest[...]

    bt_parts = split(factor(recv_b, b_sems, bt_s))
    bt_hi[...], bt_lo[...] = bt_parts
    at = factor(recv_a, a_sems, at_s)
    a_parts = split(turn(at))
    at_hi[...], at_lo[...] = split(at)
    x = mm(a_parts, bt_parts)
    sx = send_x.reshape(N * 8, C)
    for l in range(OWN):
        for rr in range(ROWS):
            for jh in range(2):
                sx[pl.ds(16 * rr * 8 + 2 * l + jh, COLS, stride=8)] = x[
                    TI * rr + 16 * l : TI * rr + 16 * (l + 1), 128 * jh : 128 * (jh + 1)
                ]
    send_all(lambda d: send_x.at[d, pl.ds(0, 4)], recv_x.at[me, pl.ds(0, 4)], x_sems)
    recv_x[me] = send_x[me]

    send_cols(lambda d: cot_view.at[:, d], cot_r.at[:, here], cot_sems)
    half_bias = COLS // 2 - 1
    waiter(bias_r.reshape(HEADS * T, T).at[pl.ds(0, HEADS * TJ * half_bias)], bias_sems).wait_recv()
    loads[5].wait()
    odd = lax.rem(c, 2)
    bias_view = bias_r.reshape(HEADS, COLS // 2, 2, TJ, T)
    pltpu.make_async_remote_copy(
        bias_view.at[:, :, odd],
        bias_view.at[:, :, odd],
        twin_sems.at[0],
        twin_sems.at[1],
        device_id=(r, c + 1 - 2 * odd),
        device_id_type=MESH,
    ).start()
    waiter(pair_r.reshape(OWN * T, C).at[pl.ds(0, OWN * TJ * (COLS - 1))], pair_sems).wait_recv()
    pair_t = turn(pair_r.reshape(OWN * T, C)[...])
    ph, ps = norm(pair_t)
    g1 = jax.nn.sigmoid(dot(w4t_s[...], right3(ph)))
    waiter(bias_r.reshape(HEADS * T, T).at[pl.ds(0, HEADS * T // 2)], twin_sems).wait_recv()
    key = lax.broadcasted_iota(jnp.int32, (T, T), 0)
    shift = jnp.where(key < valid, 0.0, -MASK_SHIFT).astype(F32)
    for h in range(HEADS):
        bias_t[h] = bias_r[h].T + shift

    waiter(recv_x.at[pl.ds(0, N - 1), pl.ds(0, 4)], x_sems).wait_recv()
    rx = recv_x.reshape(N * 8, C)
    x = jnp.concatenate([rx[pl.ds(m, C, stride=8)] for m in range(4)], axis=1)
    xh, xs = norm(x)
    m = dot(wmt_s[...], right3(xh))
    z1 = pair_t + g1 * m
    zh, zs = norm(z1)
    second = dot(w2t_s[...], right3(zh))
    score_scale = 1.0 / math.sqrt(WIDTH)
    qt_hi, qt_lo = split(second[:C] * score_scale)
    kt_hi, kt_lo = split(second[C : 2 * C])
    vt_hi, vt_lo = split(second[2 * C : 3 * C])
    g2 = jax.nn.sigmoid(second[3 * C :])
    ots = [[], []]
    inverses = [[], []]
    for l in range(OWN):
        js = slice(T * l, T * (l + 1))
        keys = head_keys(turn(second[C : 2 * C, js]))
        for h in range(HEADS):
            hs = slice(WIDTH * h, WIDTH * (h + 1))
            s = dot(keys[h], head_queries(qt_hi[:, js], qt_lo[:, js], h)) + bias_t[h]
            e = jnp.exp(s - jnp.max(s, axis=0, keepdims=True))
            inverse = 1.0 / jnp.sum(e, axis=0, keepdims=True)
            eh, el = split(e)
            e_s[l, h] = e
            e_hi[l, h] = eh
            e_lo[l, h] = el
            both = dot(jnp.concatenate([vt_hi[hs, js], vt_lo[hs, js]], axis=0), eh)
            ots[l].append((both[:WIDTH] + (both[WIDTH:] + dot(vt_hi[hs, js], el))) * inverse)
            inverses[l].append(inverse)
    o = jnp.concatenate([jnp.concatenate(ots[l], axis=0) for l in range(OWN)], axis=1)

    out_flat = out_r.reshape(OWN * T, C)
    out_flat[...] = turn(z1 + dot(wot_s[...], right3(g2 * o)))
    out_view = out_ref.reshape(OWN, TJ, TJ, C)
    send_cols(lambda d: out_r.at[:, pl.ds(pl.multiple_of(d * TJ, TJ), TJ)], out_view.at[:, c], out_sems)
    out_view[:, c] = out_r[:, here]

    for load in loads[9:]:
        load.wait()
    waiter(cot_r.reshape(OWN * T, C).at[pl.ds(0, OWN * TJ * (COLS - 1))], cot_sems).wait_recv()
    cot = turn(cot_r.reshape(OWN * T, C)[...])
    dgated = dot(wo_s[...], right3(cot))
    d_o = dgated * g2
    d_s = dgated * o * g2 * (1.0 - g2)
    dqs = [[], []]
    dks = [[], []]
    dvs = [[], []]
    for l in range(OWN):
        js = slice(T * l, T * (l + 1))
        values = head_keys(turn(second[2 * C : 3 * C, js]))
        for h in range(HEADS):
            hs = slice(WIDTH * h, WIDTH * (h + 1))
            part = d_o[hs, js] * inverses[l][h]
            delta = jnp.sum(part * ots[l][h], axis=0, keepdims=True)
            dt_hi, dt_lo = split(part)
            zero = jnp.zeros_like(dt_hi)
            blocks = [None] * HEADS
            for n, block in enumerate((dt_hi, dt_lo, dt_hi, zero)):
                blocks[(h + n) % HEADS] = block
            dp = dot(values[h], jnp.concatenate(blocks, axis=0))
            dsh, dsl = split(e_s[l, h] * (dp - delta))
            both = dot(jnp.concatenate([kt_hi[hs, js], kt_lo[hs, js]], axis=0), dsh)
            dqs[l].append(both[:WIDTH] + (both[WIDTH:] + dot(kt_hi[hs, js], dsl)))
            both = dot(jnp.concatenate([qt_hi[hs, js], qt_lo[hs, js]], axis=0), dsh, NT)
            dks[l].append(both[:WIDTH] + (both[WIDTH:] + dot(qt_hi[hs, js], dsl, NT)))
            both = dot(jnp.concatenate([dt_hi, dt_lo], axis=0), e_hi[l, h], NT)
            dvs[l].append(both[:WIDTH] + (both[WIDTH:] + dot(dt_hi, e_lo[l, h], NT)))

    def stack(parts):
        return jnp.concatenate([jnp.concatenate(parts[l], axis=0) for l in range(OWN)], axis=1)

    d_second = jnp.concatenate([stack(dqs) * score_scale, stack(dks), stack(dvs), d_s], axis=0)
    dz1 = cot + norm_back(dot(w2_s[...], right3(d_second)), zh, zs)
    dx = norm_back(dot(wm_s[...], right3(dz1 * g1)), xh, xs)
    sd = send_d.reshape(N * 8, C)
    for n in range(4):
        sd[pl.ds(n, C, stride=8)] = dx[:, 128 * n : 128 * (n + 1)]
    send_all(lambda d: send_d.at[d, pl.ds(0, 4)], recv_d.at[me, pl.ds(0, 4)], d_sems)
    recv_d[me] = send_d[me]

    grad_part = grad_r.reshape(OWN * T, C)
    dp4 = dz1 * m * g1 * (1.0 - g1)
    grad_part[...] = turn(dz1 + norm_back(dot(w4_s[...], right3(dp4)), ph, ps))
    grad_view = grad_t.reshape(OWN, TJ, TJ, C)
    send_cols(lambda d: grad_r.at[:, pl.ds(pl.multiple_of(d * TJ, TJ), TJ)], grad_view.at[:, c], grad_sems)
    grad_view[:, c] = grad_r[:, here]

    waiter(recv_d.at[pl.ds(0, N - 1), pl.ds(0, 4)], d_sems).wait_recv()
    rd = recv_d.reshape(N * 8, C)
    for l in range(OWN):
        for rr in range(ROWS):
            for jh in range(2):
                dx_s[pl.ds(TI * rr + 16 * l, 16), pl.ds(128 * jh, 128)] = rd[
                    pl.ds(16 * rr * 8 + 2 * l + jh, COLS, stride=8)
                ]
    dx_parts = split(dx_s[...])

    def send_factor(d_src, buffer, landing, sems):
        sg = buffer.reshape(N * 8, C)
        for half in range(2):
            for q in range(4):
                ys = swap_blocks(
                    [
                        d_src[(4 * q + g) * COLS : (4 * q + g + 1) * COLS, 128 * half : 128 * (half + 1)]
                        for g in range(4)
                    ]
                )
                for rr in range(4):
                    sg[pl.ds((64 * half + 16 * rr) * 8 + q, COLS, stride=8)] = ys[rr]
        send_all(lambda d: buffer.at[d, pl.ds(0, 4)], landing.at[me, pl.ds(0, 4)], sems)
        landing[me] = buffer[me]

    send_factor(mm((at_hi[...], at_lo[...]), dx_parts), send_gb, recv_gb, gb_sems)
    send_factor(mm((bt_hi[...], bt_lo[...]), dx_parts, NT), send_ga, recv_ga, ga_sems)

    def factor_back(n, landing, sems):
        waiter(landing.at[pl.ds(0, N - 1), pl.ds(0, 4)], sems).wait_recv()
        rg = landing.reshape(N * 8, C)
        d = jnp.concatenate([rg[pl.ds(q, C, stride=8)] for q in range(4)], axis=1) * mask_t[0:1]
        gate = proj_t[n]
        d_value = d * gate
        d_gate = d_value * proj_t[n + 1] * (1.0 - gate)
        return dot(w03_s[n // 2], right3(jnp.concatenate([d_gate, d_value], axis=0)))

    du = factor_back(2, recv_gb, gb_sems)
    du = du + factor_back(0, recv_ga, ga_sems)
    res = turn(norm_back(du, xhat_t[...], scale_t[0:1]))
    grad_flat = grad_ref.reshape(POS, C)
    part_flat = grad_t.reshape(POS, C)
    waiter(grad_t.at[pl.ds(0, OWN * (COLS - 1))], grad_sems).wait_recv()
    for kk in range(TJ):
        grad_flat[pl.ds(kk, TI, stride=TJ)] = res[TI * kk : TI * (kk + 1)] + part_flat[pl.ds(kk, TI, stride=TJ)]

    waiter(recv_a.at[pl.ds(0, N - 1), pl.ds(0, 4)], a_sems).wait_send()
    waiter(recv_b.at[pl.ds(0, N - 1), pl.ds(0, 4)], b_sems).wait_send()
    waiter(pair_r.reshape(OWN * T, C).at[pl.ds(0, OWN * TJ * (COLS - 1))], pair_sems).wait_send()
    waiter(cot_r.reshape(OWN * T, C).at[pl.ds(0, OWN * TJ * (COLS - 1))], cot_sems).wait_send()
    waiter(bias_r.reshape(HEADS * T, T).at[pl.ds(0, HEADS * TJ * half_bias)], bias_sems).wait_send()
    waiter(bias_r.reshape(HEADS * T, T).at[pl.ds(0, HEADS * T // 2)], twin_sems).wait_send()
    waiter(recv_ga.at[pl.ds(0, N - 1), pl.ds(0, 4)], ga_sems).wait_send()
    waiter(recv_gb.at[pl.ds(0, N - 1), pl.ds(0, 4)], gb_sems).wait_send()
    waiter(recv_x.at[pl.ds(0, N - 1), pl.ds(0, 4)], x_sems).wait_send()
    waiter(recv_d.at[pl.ds(0, N - 1), pl.ds(0, 4)], d_sems).wait_send()
    waiter(grad_t.at[pl.ds(0, OWN * (COLS - 1))], grad_sems).wait_send()
    waiter(out_ref.at[pl.ds(0, OWN * (COLS - 1))], out_sems).wait()


def body(pair, cotangent, tri_bias, valid_length, gain_first, w_first, gain_mid, w_mid, gain_second, w_second, w_att_out):
    vmem = pl.BlockSpec(memory_space=pltpu.VMEM)
    smem = pl.BlockSpec(memory_space=pltpu.SMEM)
    hbm = pl.BlockSpec(memory_space=pltpu.HBM)
    tile = pltpu.VMEM((TI, TJ, C), F32)
    message = pltpu.VMEM((N, 8, C), F32)
    weight = pltpu.VMEM((C, 3 * C), BF16)
    rows = pltpu.VMEM((OWN, T, C), F32)
    square = pltpu.VMEM((T, T), F32)
    square_low = pltpu.VMEM((T, T), BF16)
    pair_of = pltpu.SemaphoreType.DMA((2,))
    return pl.pallas_call(
        kernel,
        out_shape=(tile, tile),
        in_specs=[smem] + [hbm] * 10,
        out_specs=(vmem, vmem),
        scratch_shapes=[
            message,
            message,
            message,
            message,
            message,
            message,
            message,
            message,
            message,
            message,
            message,
            message,
            rows,
            rows,
            pltpu.VMEM((HEADS, T, T), F32),
            pltpu.VMEM((HEADS, T, T), F32),
            rows,
            rows,
            pltpu.VMEM((TI, TJ, C), F32),
            pltpu.VMEM((C, POS), F32),
            pltpu.VMEM((8, POS), F32),
            pltpu.VMEM((4, C, POS), F32),
            pltpu.VMEM((8, POS), F32),
            square,
            square,
            square_low,
            square_low,
            square_low,
            square_low,
            square,
            pltpu.VMEM((OWN, HEADS, T, T), F32),
            pltpu.VMEM((OWN, HEADS, T, T), BF16),
            pltpu.VMEM((OWN, HEADS, T, T), BF16),
            pltpu.VMEM((2, C, 6 * C), BF16),
            weight,
            weight,
            weight,
            weight,
            weight,
            weight,
            pltpu.VMEM((C, 12 * C), BF16),
            pltpu.VMEM((4 * C, 3 * C), BF16),
            pltpu.VMEM((TI, TJ, C), F32),
            pltpu.VMEM((C, 5 * C), F32),
            pltpu.VMEM((C, C), F32),
            pltpu.VMEM((C, 4 * C), F32),
            pltpu.VMEM((C, C), F32),
            pltpu.VMEM((1, C), F32),
            pltpu.VMEM((1, C), F32),
            pltpu.VMEM((1, C), F32),
            pltpu.SemaphoreType.REGULAR,
            pltpu.SemaphoreType.DMA((10,)),
            pair_of,
            pair_of,
            pair_of,
            pair_of,
            pair_of,
            pair_of,
            pair_of,
            pair_of,
            pair_of,
            pair_of,
            pair_of,
            pair_of,
        ],
        compiler_params=pltpu.CompilerParams(
            collective_id=0, has_side_effects=True, vmem_limit_bytes=48 * 1024 * 1024
        ),
        cost_estimate=pl.CostEstimate(flops=2_000_000_000, bytes_accessed=4_000_000, transcendentals=1_000_000),
    )(
        valid_length,
        *(
            pltpu.with_memory_space_constraint(operand, pltpu.HBM)
            for operand in (
                pair,
                cotangent,
                tri_bias,
                gain_first.reshape(1, C),
                w_first,
                gain_mid.reshape(1, C),
                w_mid,
                gain_second.reshape(1, C),
                w_second,
                w_att_out,
            )
        ),
    )


def solution(mesh):
    return jax.shard_map(
        body,
        mesh=mesh,
        in_specs=(
            P("row", "col", None),
            P("row", "col", None),
            P(None, "col", None),
            P(),
            P(),
            P(),
            P(),
            P(),
            P(),
            P(),
            P(),
        ),
        out_specs=(P("row", "col", None), P("row", "col", None)),
        check_vma=False,
    )
```

```python
import itertools
import math

import jax
import jax.numpy as jnp
from jax import lax
from jax.experimental import pallas as pl
from jax.experimental.pallas import tpu as pltpu
from jax.sharding import PartitionSpec as P

EPSILON = 1e-05
MASK_SHIFT = 1000000000.0
MESH = pl.DeviceIdType.MESH
LOGICAL = pl.DeviceIdType.LOGICAL
F32 = jnp.float32
BF16 = jnp.bfloat16
NN = (((1,), (0,)), ((), ()))
NT = (((1,), (1,)), ((), ()))

T = 256
C = 128
HEADS = 4
WIDTH = 32
ROWS = 8
COLS = 16
N = ROWS * COLS
TI = T // ROWS
TJ = T // COLS
POS = TI * TJ
OWN = T // N


def split(x):
    hi = x.astype(BF16)
    return hi, (x - hi.astype(F32)).astype(BF16)


def dot(a, b, dims=NN):
    return lax.dot_general(a, b, dims, preferred_element_type=F32)


def mm(a, b, dims=NN):
    return dot(a[0], b[0], dims) + (dot(a[0], b[1], dims) + dot(a[1], b[0], dims))


def norm(u):
    centre = u - jnp.mean(u, axis=0, keepdims=True)
    scale = lax.rsqrt(jnp.mean(centre * centre, axis=0, keepdims=True) + EPSILON)
    return centre * scale, scale


def norm_back(d, xhat, scale):
    mean_d = jnp.mean(d, axis=0, keepdims=True)
    mean_dx = jnp.mean(d * xhat, axis=0, keepdims=True)
    return scale * (d - mean_d - xhat * mean_dx)


def left3(x):
    hi, lo = split(x)
    return jnp.concatenate([hi, lo, hi], axis=1)


def right3(x):
    hi, lo = split(x)
    return jnp.concatenate([hi, hi, lo], axis=0)


def turn(x):
    rows, cols = x.shape
    return jnp.concatenate(
        [
            jnp.concatenate([x[128 * i : 128 * (i + 1), 128 * j : 128 * (j + 1)].T for i in range(rows // 128)], axis=1)
            for j in range(cols // 128)
        ],
        axis=0,
    )


def swap_blocks(xs):
    block = lax.broadcasted_iota(jnp.int32, xs[0].shape, 1) // 32
    for bit in (2, 1):
        upper = (block & bit) != 0
        ys = list(xs)
        for s in range(4):
            if s & bit == 0:
                a, b = xs[s], xs[s | bit]
                ys[s] = jnp.where(upper, pltpu.roll(b, 32 * bit, 1), a)
                ys[s | bit] = jnp.where(upper, b, pltpu.roll(a, 128 - 32 * bit, 1))
        xs = ys
    return xs


def head_keys(x):
    hi = x.astype(BF16).astype(F32)
    again = pltpu.roll(hi, WIDTH, 1)
    lo = pltpu.roll(x - hi, 2 * WIDTH, 1)
    block = lax.broadcasted_iota(jnp.int32, x.shape, 1) // WIDTH
    return [
        jnp.where(block == h, hi, jnp.where(block == (h + 1) % HEADS, again, lo)).astype(BF16) for h in range(HEADS)
    ]


def head_queries(hi, lo, h):
    own = slice(WIDTH * h, WIDTH * (h + 1))
    blocks = [None] * HEADS
    blocks[h] = hi[own]
    blocks[(h + 1) % HEADS] = lo[own]
    blocks[(h + 2) % HEADS] = hi[own]
    blocks[(h + 3) % HEADS] = jnp.zeros_like(hi[own])
    return jnp.concatenate(blocks, axis=0)


def kernel(
    valid_ref,
    pair_any,
    cot_any,
    bias_any,
    gain_first_any,
    w_first_any,
    gain_mid_any,
    w_mid_any,
    gain_second_any,
    w_second_any,
    w_att_out_any,
    out_ref,
    grad_ref,
    send_a,
    recv_a,
    send_b,
    recv_b,
    send_x,
    recv_x,
    send_d,
    recv_d,
    send_ga,
    recv_ga,
    send_gb,
    recv_gb,
    pair_r,
    cot_r,
    bias_r,
    bias_t,
    out_r,
    grad_r,
    grad_t,
    xhat_t,
    scale_t,
    proj_t,
    mask_t,
    at_s,
    bt_s,
    at_hi,
    at_lo,
    bt_hi,
    bt_lo,
    dx_s,
    e_s,
    e_hi,
    e_lo,
    w03_s,
    w4_s,
    w4t_s,
    wm_s,
    wmt_s,
    wo_s,
    wot_s,
    w2_s,
    w2t_s,
    pair_ref,
    w_first,
    w_mid,
    w_second,
    w_att_out,
    gain_first,
    gain_mid,
    gain_second,
    load_sems,
    a_sems,
    b_sems,
    x_sems,
    d_sems,
    ga_sems,
    gb_sems,
    pair_sems,
    cot_sems,
    bias_sems,
    twin_sems,
    out_sems,
    grad_sems,
):
    r = lax.axis_index("row")
    c = lax.axis_index("col")
    me = r * COLS + c
    valid = valid_ref[0]

    barrier = pltpu.get_barrier_semaphore()

    here = pl.ds(pl.multiple_of(c * TJ, TJ), TJ)
    cot_view = cot_any.reshape(OWN, TJ, TJ, C)
    loads = [
        pltpu.make_async_copy(src, dst, load_sems.at[n])
        for n, (src, dst) in enumerate(
            (
                (pair_any, pair_ref),
                (w_first_any, w_first),
                (gain_first_any, gain_first),
                (gain_mid_any, gain_mid),
                (gain_second_any, gain_second),
                (bias_any, bias_r.at[:, here]),
                (w_second_any, w_second),
                (w_mid_any, w_mid),
                (w_att_out_any, w_att_out),
                (cot_view.at[:, c], cot_r.at[:, here]),
            )
        )
    ]
    for load in loads:
        load.start()

    x_at = lax.rem(lax.div(c, 2), 2) * 2 + lax.div(r, 4)
    xs_at = [lax.rem(x_at + n, 4) for n in range(4)]
    of_x = [4 * COLS * lax.rem(v, 2) + 2 * lax.div(v, 2) for v in xs_at]
    of_y = [COLS * lax.rem(lax.rem(r, 4) + n, 4) for n in range(4)]
    of_z = [4 * lax.rem(lax.div(c, 4) + n, 4) for n in range(4)]
    own_core = lax.rem(c, 2)
    other_core = 1 - 2 * own_core
    own_hi = 2 * lax.rem(lax.div(c, 2), 2)
    of_hi = [own_hi, 2 - own_hi]

    def for_all(visit):
        for hops in sorted(itertools.product(range(3), repeat=3), key=lambda h: -sum(h)):
            ones = [axis for axis in range(3) if hops[axis] == 1]

            def go(t, _):
                def pick(options, axis):
                    if axis not in ones:
                        return options[hops[axis]]
                    sign = lax.rem(lax.div(t, 2 ** (1 + ones.index(axis))), 2)
                    return options[1] + sign * (options[3] - options[1])

                core = own_core + lax.rem(t, 2) * other_core
                visit((pick(of_x, 0) + pick(of_y, 1)) + (pick(of_z, 2) + core))
                return 0

            lax.fori_loop(0 if sum(hops) else 1, 2 ** (1 + len(ones)), go, 0, unroll=True)

    def for_cols(visit, cores=2):
        for hi, z in ((1, 2), (1, 1), (1, 3), (0, 2), (1, 0), (0, 1), (0, 3), (0, 0)):

            def go(t, _):
                visit(of_hi[hi] + of_z[z] + (own_core + t * other_core))
                return 0

            if hi + z:
                lax.fori_loop(0, cores, go, 0, unroll=True)
            elif cores == 2:
                go(1, 0)

    def send_all(src, dst, sems):
        def visit(d):
            pltpu.make_async_remote_copy(
                src(d), dst, sems.at[0], sems.at[1], device_id=d, device_id_type=LOGICAL
            ).start()

        for_all(visit)

    def send_cols(src, dst, sems, cores=2):
        def visit(d):
            pltpu.make_async_remote_copy(
                src(d), dst, sems.at[0], sems.at[1], device_id=r * COLS + d, device_id_type=LOGICAL
            ).start()

        for_cols(visit, cores)

    def greet(d):
        pl.semaphore_signal(barrier, inc=1, device_id=d, device_id_type=LOGICAL)

    for_all(greet)

    def waiter(view, sems):
        return pltpu.make_async_remote_copy(view, view, sems.at[0], sems.at[1], device_id=(r, c), device_id_type=MESH)

    for load in loads[:3]:
        load.wait()
    pair_flat = pair_ref.reshape(POS, C)
    u = jnp.concatenate(
        [
            jnp.concatenate([pair_flat[pl.ds(4 * q + g, TI, stride=TJ)] for g in range(4)], axis=0).T
            for q in range(4)
        ],
        axis=1,
    )
    xhat, scale = norm(u)
    xhat_t[...] = xhat
    scale_t[...] = jnp.broadcast_to(scale, (8, POS))
    gain = jnp.broadcast_to(gain_first[...], (C, C)).T
    w03 = w_first[:, : 4 * C] * jnp.concatenate([gain] * 4, axis=1)
    w03_s[0] = left3(w03[:, : 2 * C])
    w03_s[1] = left3(w03[:, 2 * C :])
    proj = dot(left3(turn(w03)), right3(xhat))
    pos = lax.broadcasted_iota(jnp.int32, (8, POS), 1)
    in_row = (r * TI + pos % TI) < valid
    in_col = (c * TJ + pos // TI) < valid
    mask_t[...] = jnp.where(in_row & in_col, 1.0, 0.0).astype(F32)
    mask = mask_t[0:1]
    sig0 = jax.nn.sigmoid(proj[:C])
    sig2 = jax.nn.sigmoid(proj[2 * C : 3 * C])
    p1 = proj[C : 2 * C]
    p3 = proj[3 * C :]
    proj_t[0] = sig0
    proj_t[1] = p1
    proj_t[2] = sig2
    proj_t[3] = p3
    left = mask * sig0 * p1
    right = mask * sig2 * p3
    sa = send_a.reshape(N * 8, C)
    sb = send_b.reshape(N * 8, C)
    for q in range(4):
        sa[pl.ds(q, C, stride=8)] = left[:, 128 * q : 128 * (q + 1)]
        sb[pl.ds(q, C, stride=8)] = right[:, 128 * q : 128 * (q + 1)]


    pl.semaphore_wait(barrier, N - 1)
    send_all(lambda d: send_b.at[d, pl.ds(0, 4)], recv_b.at[me, pl.ds(0, 4)], b_sems)
    recv_b[me] = send_b[me]
    send_all(lambda d: send_a.at[d, pl.ds(0, 4)], recv_a.at[me, pl.ds(0, 4)], a_sems)
    recv_a[me] = send_a[me]

    pair_view = pair_ref.reshape(OWN, TJ, TJ, C)

    send_cols(lambda d: bias_any, bias_r.at[:, here], bias_sems, cores=1)
    send_cols(lambda d: pair_view.at[:, d], pair_r.at[:, here], pair_sems)
    pair_r[:, here] = pair_view[:, c]

    for load in loads[3:5] + loads[6:9]:
        load.wait()
    w4 = w_first[:, 4 * C :] * gain
    w4_s[...] = left3(w4)
    w4t_s[...] = left3(w4.T)
    w_m = w_mid[...] * jnp.broadcast_to(gain_mid[...], (C, C)).T
    wm_s[...] = left3(w_m)
    wmt_s[...] = left3(w_m.T)
    wo_s[...] = left3(w_att_out[...])
    wot_s[...] = left3(w_att_out[...].T)
    w_sec = w_second[...] * jnp.concatenate([jnp.broadcast_to(gain_second[...], (C, C)).T] * 4, axis=1)
    w2_s[...] = left3(w_sec)
    w2t_s[...] = left3(turn(w_sec))

    def factor(landing, sems, dest):
        waiter(landing.at[pl.ds(0, N - 1), pl.ds(0, 4)], sems).wait_recv()
        ra = landing.reshape(N * 8, C)
        for half in range(2):
            for q in range(4):
                ys = swap_blocks([ra[pl.ds((64 * half + 16 * rr) * 8 + q, COLS, stride=8)] for rr in range(4)])
                for g in range(4):
                    dest[pl.ds((4 * q + g) * COLS, COLS), pl.ds(128 * half, 128)] = ys[g]
        return dest[...]

    bt_parts = split(factor(recv_b, b_sems, bt_s))
    bt_hi[...], bt_lo[...] = bt_parts
    at = factor(recv_a, a_sems, at_s)
    a_parts = split(turn(at))
    at_hi[...], at_lo[...] = split(at)
    x = mm(a_parts, bt_parts)
    sx = send_x.reshape(N * 8, C)
    for l in range(OWN):
        for rr in range(ROWS):
            for jh in range(2):
                sx[pl.ds(16 * rr * 8 + 2 * l + jh, COLS, stride=8)] = x[
                    TI * rr + 16 * l : TI * rr + 16 * (l + 1), 128 * jh : 128 * (jh + 1)
                ]
    send_all(lambda d: send_x.at[d, pl.ds(0, 4)], recv_x.at[me, pl.ds(0, 4)], x_sems)
    recv_x[me] = send_x[me]

    send_cols(lambda d: cot_view.at[:, d], cot_r.at[:, here], cot_sems)
    half_bias = COLS // 2 - 1
    waiter(bias_r.reshape(HEADS * T, T).at[pl.ds(0, HEADS * TJ * half_bias)], bias_sems).wait_recv()
    loads[5].wait()
    odd = lax.rem(c, 2)
    bias_view = bias_r.reshape(HEADS, COLS // 2, 2, TJ, T)
    pltpu.make_async_remote_copy(
        bias_view.at[:, :, odd],
        bias_view.at[:, :, odd],
        twin_sems.at[0],
        twin_sems.at[1],
        device_id=(r, c + 1 - 2 * odd),
        device_id_type=MESH,
    ).start()
    waiter(pair_r.reshape(OWN * T, C).at[pl.ds(0, OWN * TJ * (COLS - 1))], pair_sems).wait_recv()
    pair_t = turn(pair_r.reshape(OWN * T, C)[...])
    ph, ps = norm(pair_t)
    g1 = jax.nn.sigmoid(dot(w4t_s[...], right3(ph)))
    waiter(bias_r.reshape(HEADS * T, T).at[pl.ds(0, HEADS * T // 2)], twin_sems).wait_recv()
    key = lax.broadcasted_iota(jnp.int32, (T, T), 0)
    shift = jnp.where(key < valid, 0.0, -MASK_SHIFT).astype(F32)
    for h in range(HEADS):
        bias_t[h] = bias_r[h].T + shift

    waiter(recv_x.at[pl.ds(0, N - 1), pl.ds(0, 4)], x_sems).wait_recv()
    rx = recv_x.reshape(N * 8, C)
    x = jnp.concatenate([rx[pl.ds(m, C, stride=8)] for m in range(4)], axis=1)
    xh, xs = norm(x)
    m = dot(wmt_s[...], right3(xh))
    z1 = pair_t + g1 * m
    zh, zs = norm(z1)
    second = dot(w2t_s[...], right3(zh))
    score_scale = 1.0 / math.sqrt(WIDTH)
    qt_hi, qt_lo = split(second[:C] * score_scale)
    kt_hi, kt_lo = split(second[C : 2 * C])
    vt_hi, vt_lo = split(second[2 * C : 3 * C])
    g2 = jax.nn.sigmoid(second[3 * C :])
    ots = [[], []]
    inverses = [[], []]
    all_keys = [head_keys(turn(second[C : 2 * C, T * l : T * (l + 1)])) for l in range(OWN)]
    for h in range(HEADS):
        hs = slice(WIDTH * h, WIDTH * (h + 1))
        for l in range(OWN):
            js = slice(T * l, T * (l + 1))
            keys = all_keys[l]
            s = dot(keys[h], head_queries(qt_hi[:, js], qt_lo[:, js], h)) + bias_t[h]
            e = jnp.exp(s - jnp.max(s, axis=0, keepdims=True))
            inverse = 1.0 / jnp.sum(e, axis=0, keepdims=True)
            eh, el = split(e)
            e_s[l, h] = e
            e_hi[l, h] = eh
            e_lo[l, h] = el
            both = dot(jnp.concatenate([vt_hi[hs, js], vt_lo[hs, js]], axis=0), eh)
            ots[l].append((both[:WIDTH] + (both[WIDTH:] + dot(vt_hi[hs, js], el))) * inverse)
            inverses[l].append(inverse)
    o = jnp.concatenate([jnp.concatenate(ots[l], axis=0) for l in range(OWN)], axis=1)

    out_flat = out_r.reshape(OWN * T, C)
    out_flat[...] = turn(z1 + dot(wot_s[...], right3(g2 * o)))
    out_view = out_ref.reshape(OWN, TJ, TJ, C)
    send_cols(lambda d: out_r.at[:, pl.ds(pl.multiple_of(d * TJ, TJ), TJ)], out_view.at[:, c], out_sems)
    out_view[:, c] = out_r[:, here]

    for load in loads[9:]:
        load.wait()
    waiter(cot_r.reshape(OWN * T, C).at[pl.ds(0, OWN * TJ * (COLS - 1))], cot_sems).wait_recv()
    cot = turn(cot_r.reshape(OWN * T, C)[...])
    dgated = dot(wo_s[...], right3(cot))
    d_o = dgated * g2
    d_s = dgated * o * g2 * (1.0 - g2)
    dqs = [[], []]
    dks = [[], []]
    dvs = [[], []]
    all_values = [head_keys(turn(second[2 * C : 3 * C, T * l : T * (l + 1)])) for l in range(OWN)]
    for h in range(HEADS):
        hs = slice(WIDTH * h, WIDTH * (h + 1))
        for l in range(OWN):
            js = slice(T * l, T * (l + 1))
            values = all_values[l]
            part = d_o[hs, js] * inverses[l][h]
            delta = jnp.sum(part * ots[l][h], axis=0, keepdims=True)
            dt_hi, dt_lo = split(part)
            zero = jnp.zeros_like(dt_hi)
            blocks = [None] * HEADS
            for n, block in enumerate((dt_hi, dt_lo, dt_hi, zero)):
                blocks[(h + n) % HEADS] = block
            dp = dot(values[h], jnp.concatenate(blocks, axis=0))
            dsh, dsl = split(e_s[l, h] * (dp - delta))
            both = dot(jnp.concatenate([kt_hi[hs, js], kt_lo[hs, js]], axis=0), dsh)
            dqs[l].append(both[:WIDTH] + (both[WIDTH:] + dot(kt_hi[hs, js], dsl)))
            both = dot(jnp.concatenate([qt_hi[hs, js], qt_lo[hs, js]], axis=0), dsh, NT)
            dks[l].append(both[:WIDTH] + (both[WIDTH:] + dot(qt_hi[hs, js], dsl, NT)))
            both = dot(jnp.concatenate([dt_hi, dt_lo], axis=0), e_hi[l, h], NT)
            dvs[l].append(both[:WIDTH] + (both[WIDTH:] + dot(dt_hi, e_lo[l, h], NT)))

    def stack(parts):
        return jnp.concatenate([jnp.concatenate(parts[l], axis=0) for l in range(OWN)], axis=1)

    d_second = jnp.concatenate([stack(dqs) * score_scale, stack(dks), stack(dvs), d_s], axis=0)
    dz1 = cot + norm_back(dot(w2_s[...], right3(d_second)), zh, zs)
    dx = norm_back(dot(wm_s[...], right3(dz1 * g1)), xh, xs)
    sd = send_d.reshape(N * 8, C)
    for n in range(4):
        sd[pl.ds(n, C, stride=8)] = dx[:, 128 * n : 128 * (n + 1)]
    send_all(lambda d: send_d.at[d, pl.ds(0, 4)], recv_d.at[me, pl.ds(0, 4)], d_sems)
    recv_d[me] = send_d[me]

    grad_part = grad_r.reshape(OWN * T, C)
    dp4 = dz1 * m * g1 * (1.0 - g1)
    grad_part[...] = turn(dz1 + norm_back(dot(w4_s[...], right3(dp4)), ph, ps))
    grad_view = grad_t.reshape(OWN, TJ, TJ, C)
    send_cols(lambda d: grad_r.at[:, pl.ds(pl.multiple_of(d * TJ, TJ), TJ)], grad_view.at[:, c], grad_sems)
    grad_view[:, c] = grad_r[:, here]

    waiter(recv_d.at[pl.ds(0, N - 1), pl.ds(0, 4)], d_sems).wait_recv()
    rd = recv_d.reshape(N * 8, C)
    for l in range(OWN):
        for rr in range(ROWS):
            for jh in range(2):
                dx_s[pl.ds(TI * rr + 16 * l, 16), pl.ds(128 * jh, 128)] = rd[
                    pl.ds(16 * rr * 8 + 2 * l + jh, COLS, stride=8)
                ]
    dx_parts = split(dx_s[...])

    def send_factor(d_src, buffer, landing, sems):
        sg = buffer.reshape(N * 8, C)
        for half in range(2):
            for q in range(4):
                ys = swap_blocks(
                    [
                        d_src[(4 * q + g) * COLS : (4 * q + g + 1) * COLS, 128 * half : 128 * (half + 1)]
                        for g in range(4)
                    ]
                )
                for rr in range(4):
                    sg[pl.ds((64 * half + 16 * rr) * 8 + q, COLS, stride=8)] = ys[rr]
        send_all(lambda d: buffer.at[d, pl.ds(0, 4)], landing.at[me, pl.ds(0, 4)], sems)
        landing[me] = buffer[me]

    send_factor(mm((at_hi[...], at_lo[...]), dx_parts), send_gb, recv_gb, gb_sems)
    send_factor(mm((bt_hi[...], bt_lo[...]), dx_parts, NT), send_ga, recv_ga, ga_sems)

    def factor_back(n, landing, sems):
        waiter(landing.at[pl.ds(0, N - 1), pl.ds(0, 4)], sems).wait_recv()
        rg = landing.reshape(N * 8, C)
        d = jnp.concatenate([rg[pl.ds(q, C, stride=8)] for q in range(4)], axis=1) * mask_t[0:1]
        gate = proj_t[n]
        d_value = d * gate
        d_gate = d_value * proj_t[n + 1] * (1.0 - gate)
        return dot(w03_s[n // 2], right3(jnp.concatenate([d_gate, d_value], axis=0)))

    du = factor_back(2, recv_gb, gb_sems)
    du = du + factor_back(0, recv_ga, ga_sems)
    res = turn(norm_back(du, xhat_t[...], scale_t[0:1]))
    grad_flat = grad_ref.reshape(POS, C)
    part_flat = grad_t.reshape(POS, C)
    waiter(grad_t.at[pl.ds(0, OWN * (COLS - 1))], grad_sems).wait_recv()
    for kk in range(TJ):
        grad_flat[pl.ds(kk, TI, stride=TJ)] = res[TI * kk : TI * (kk + 1)] + part_flat[pl.ds(kk, TI, stride=TJ)]

    waiter(recv_a.at[pl.ds(0, N - 1), pl.ds(0, 4)], a_sems).wait_send()
    waiter(recv_b.at[pl.ds(0, N - 1), pl.ds(0, 4)], b_sems).wait_send()
    waiter(pair_r.reshape(OWN * T, C).at[pl.ds(0, OWN * TJ * (COLS - 1))], pair_sems).wait_send()
    waiter(cot_r.reshape(OWN * T, C).at[pl.ds(0, OWN * TJ * (COLS - 1))], cot_sems).wait_send()
    waiter(bias_r.reshape(HEADS * T, T).at[pl.ds(0, HEADS * TJ * half_bias)], bias_sems).wait_send()
    waiter(bias_r.reshape(HEADS * T, T).at[pl.ds(0, HEADS * T // 2)], twin_sems).wait_send()
    waiter(recv_ga.at[pl.ds(0, N - 1), pl.ds(0, 4)], ga_sems).wait_send()
    waiter(recv_gb.at[pl.ds(0, N - 1), pl.ds(0, 4)], gb_sems).wait_send()
    waiter(recv_x.at[pl.ds(0, N - 1), pl.ds(0, 4)], x_sems).wait_send()
    waiter(recv_d.at[pl.ds(0, N - 1), pl.ds(0, 4)], d_sems).wait_send()
    waiter(grad_t.at[pl.ds(0, OWN * (COLS - 1))], grad_sems).wait_send()
    waiter(out_ref.at[pl.ds(0, OWN * (COLS - 1))], out_sems).wait()


def store(out_ref, grad_ref, out_any, grad_any, sems):
    copies = [
        pltpu.make_async_copy(out_ref, out_any, sems.at[0]),
        pltpu.make_async_copy(grad_ref, grad_any, sems.at[1]),
    ]
    for copy in copies:
        copy.start()
    for copy in copies:
        copy.wait()


def body(pair, cotangent, tri_bias, valid_length, gain_first, w_first, gain_mid, w_mid, gain_second, w_second, w_att_out):
    vmem = pl.BlockSpec(memory_space=pltpu.VMEM)
    smem = pl.BlockSpec(memory_space=pltpu.SMEM)
    hbm = pl.BlockSpec(memory_space=pltpu.HBM)
    tile = pltpu.VMEM((TI, TJ, C), F32)
    message = pltpu.VMEM((N, 8, C), F32)
    weight = pltpu.VMEM((C, 3 * C), BF16)
    rows = pltpu.VMEM((OWN, T, C), F32)
    square = pltpu.VMEM((T, T), F32)
    square_low = pltpu.VMEM((T, T), BF16)
    pair_of = pltpu.SemaphoreType.DMA((2,))
    results = pl.pallas_call(
        kernel,
        out_shape=(tile, tile),
        in_specs=[smem] + [hbm] * 10,
        out_specs=(vmem, vmem),
        scratch_shapes=[
            message,
            message,
            message,
            message,
            message,
            message,
            message,
            message,
            message,
            message,
            message,
            message,
            rows,
            rows,
            pltpu.VMEM((HEADS, T, T), F32),
            pltpu.VMEM((HEADS, T, T), F32),
            rows,
            rows,
            pltpu.VMEM((TI, TJ, C), F32),
            pltpu.VMEM((C, POS), F32),
            pltpu.VMEM((8, POS), F32),
            pltpu.VMEM((4, C, POS), F32),
            pltpu.VMEM((8, POS), F32),
            square,
            square,
            square_low,
            square_low,
            square_low,
            square_low,
            square,
            pltpu.VMEM((OWN, HEADS, T, T), F32),
            pltpu.VMEM((OWN, HEADS, T, T), BF16),
            pltpu.VMEM((OWN, HEADS, T, T), BF16),
            pltpu.VMEM((2, C, 6 * C), BF16),
            weight,
            weight,
            weight,
            weight,
            weight,
            weight,
            pltpu.VMEM((C, 12 * C), BF16),
            pltpu.VMEM((4 * C, 3 * C), BF16),
            pltpu.VMEM((TI, TJ, C), F32),
            pltpu.VMEM((C, 5 * C), F32),
            pltpu.VMEM((C, C), F32),
            pltpu.VMEM((C, 4 * C), F32),
            pltpu.VMEM((C, C), F32),
            pltpu.VMEM((1, C), F32),
            pltpu.VMEM((1, C), F32),
            pltpu.VMEM((1, C), F32),
            pltpu.SemaphoreType.DMA((10,)),
            pair_of,
            pair_of,
            pair_of,
            pair_of,
            pair_of,
            pair_of,
            pair_of,
            pair_of,
            pair_of,
            pair_of,
            pair_of,
            pair_of,
        ],
        compiler_params=pltpu.CompilerParams(
            collective_id=0, has_side_effects=True, vmem_limit_bytes=48 * 1024 * 1024
        ),
        cost_estimate=pl.CostEstimate(flops=2_000_000_000, bytes_accessed=4_000_000, transcendentals=1_000_000),
    )(
        valid_length,
        *(
            pltpu.with_memory_space_constraint(operand, pltpu.HBM)
            for operand in (
                pair,
                cotangent,
                tri_bias,
                gain_first.reshape(1, C),
                w_first,
                gain_mid.reshape(1, C),
                w_mid,
                gain_second.reshape(1, C),
                w_second,
                w_att_out,
            )
        ),
    )
    whole = jax.ShapeDtypeStruct((TI, TJ, C), F32)
    anywhere = pl.BlockSpec(memory_space=pl.ANY)
    return pl.pallas_call(
        store,
        out_shape=(whole, whole),
        in_specs=[anywhere, anywhere],
        out_specs=(anywhere, anywhere),
        scratch_shapes=[pltpu.SemaphoreType.DMA((2,))],
        compiler_params=pltpu.CompilerParams(vmem_limit_bytes=16 * 1024 * 1024),
    )(*(pltpu.with_memory_space_constraint(result, pltpu.VMEM) for result in results))


def solution(mesh):
    return jax.shard_map(
        body,
        mesh=mesh,
        in_specs=(
            P("row", "col", None),
            P("row", "col", None),
            P(None, "col", None),
            P(),
            P(),
            P(),
            P(),
            P(),
            P(),
            P(),
            P(),
        ),
        out_specs=(P("row", "col", None), P("row", "col", None)),
        check_vma=False,
    )
```

```python
import itertools
import math

import jax
import jax.numpy as jnp
from jax import lax
from jax.experimental import pallas as pl
from jax.experimental.pallas import tpu as pltpu
from jax.sharding import PartitionSpec as P

EPSILON = 1e-05
MASK_SHIFT = 1000000000.0
MESH = pl.DeviceIdType.MESH
LOGICAL = pl.DeviceIdType.LOGICAL
F32 = jnp.float32
BF16 = jnp.bfloat16
NN = (((1,), (0,)), ((), ()))
NT = (((1,), (1,)), ((), ()))

T = 256
C = 128
HEADS = 4
WIDTH = 32
ROWS = 8
COLS = 16
N = ROWS * COLS
TI = T // ROWS
TJ = T // COLS
POS = TI * TJ
OWN = T // N


def split(x):
    hi = x.astype(BF16)
    return hi, (x - hi.astype(F32)).astype(BF16)


def dot(a, b, dims=NN):
    return lax.dot_general(a, b, dims, preferred_element_type=F32)


def mm(a, b, dims=NN):
    return dot(a[0], b[0], dims) + (dot(a[0], b[1], dims) + dot(a[1], b[0], dims))


def norm(u):
    centre = u - jnp.mean(u, axis=0, keepdims=True)
    scale = lax.rsqrt(jnp.mean(centre * centre, axis=0, keepdims=True) + EPSILON)
    return centre * scale, scale


def norm_back(d, xhat, scale):
    mean_d = jnp.mean(d, axis=0, keepdims=True)
    mean_dx = jnp.mean(d * xhat, axis=0, keepdims=True)
    return scale * (d - mean_d - xhat * mean_dx)


def left3(x):
    hi, lo = split(x)
    return jnp.concatenate([hi, lo, hi], axis=1)


def right3(x):
    hi, lo = split(x)
    return jnp.concatenate([hi, hi, lo], axis=0)


def turn(x):
    rows, cols = x.shape
    return jnp.concatenate(
        [
            jnp.concatenate([x[128 * i : 128 * (i + 1), 128 * j : 128 * (j + 1)].T for i in range(rows // 128)], axis=1)
            for j in range(cols // 128)
        ],
        axis=0,
    )


def swap_blocks(xs):
    block = lax.broadcasted_iota(jnp.int32, xs[0].shape, 1) // 32
    for bit in (2, 1):
        upper = (block & bit) != 0
        ys = list(xs)
        for s in range(4):
            if s & bit == 0:
                a, b = xs[s], xs[s | bit]
                ys[s] = jnp.where(upper, pltpu.roll(b, 32 * bit, 1), a)
                ys[s | bit] = jnp.where(upper, b, pltpu.roll(a, 128 - 32 * bit, 1))
        xs = ys
    return xs


def head_keys(x):
    hi = x.astype(BF16).astype(F32)
    again = pltpu.roll(hi, WIDTH, 1)
    lo = pltpu.roll(x - hi, 2 * WIDTH, 1)
    block = lax.broadcasted_iota(jnp.int32, x.shape, 1) // WIDTH
    return [
        jnp.where(block == h, hi, jnp.where(block == (h + 1) % HEADS, again, lo)).astype(BF16) for h in range(HEADS)
    ]


def head_queries(hi, lo, h):
    own = slice(WIDTH * h, WIDTH * (h + 1))
    blocks = [None] * HEADS
    blocks[h] = hi[own]
    blocks[(h + 1) % HEADS] = lo[own]
    blocks[(h + 2) % HEADS] = hi[own]
    blocks[(h + 3) % HEADS] = jnp.zeros_like(hi[own])
    return jnp.concatenate(blocks, axis=0)


def kernel(
    valid_ref,
    pair_any,
    cot_any,
    bias_any,
    gain_first_any,
    w_first_any,
    gain_mid_any,
    w_mid_any,
    gain_second_any,
    w_second_any,
    w_att_out_any,
    out_ref,
    grad_ref,
    send_a,
    recv_a,
    send_b,
    recv_b,
    send_x,
    recv_x,
    send_d,
    recv_d,
    send_ga,
    recv_ga,
    send_gb,
    recv_gb,
    pair_r,
    cot_r,
    bias_r,
    bias_t,
    out_r,
    grad_r,
    grad_t,
    xhat_t,
    scale_t,
    proj_t,
    mask_t,
    at_s,
    bt_s,
    at_hi,
    at_lo,
    bt_hi,
    bt_lo,
    dx_s,
    e_s,
    e_hi,
    e_lo,
    w03_s,
    w4_s,
    w4t_s,
    wm_s,
    wmt_s,
    wo_s,
    wot_s,
    w2_s,
    w2t_s,
    pair_ref,
    w_first,
    w_mid,
    w_second,
    w_att_out,
    gain_first,
    gain_mid,
    gain_second,
    load_sems,
    a_sems,
    b_sems,
    x_sems,
    d_sems,
    ga_sems,
    gb_sems,
    pair_sems,
    cot_sems,
    bias_sems,
    twin_sems,
    out_sems,
    grad_sems,
):
    r = lax.axis_index("row")
    c = lax.axis_index("col")
    me = r * COLS + c
    valid = valid_ref[0]

    barrier = pltpu.get_barrier_semaphore()

    here = pl.ds(pl.multiple_of(c * TJ, TJ), TJ)
    cot_view = cot_any.reshape(OWN, TJ, TJ, C)
    loads = [
        pltpu.make_async_copy(src, dst, load_sems.at[n])
        for n, (src, dst) in enumerate(
            (
                (pair_any, pair_ref),
                (w_first_any, w_first),
                (gain_first_any, gain_first),
                (gain_mid_any, gain_mid),
                (gain_second_any, gain_second),
                (bias_any, bias_r.at[:, here]),
                (w_second_any, w_second),
                (w_mid_any, w_mid),
                (w_att_out_any, w_att_out),
                (cot_view.at[:, c], cot_r.at[:, here]),
            )
        )
    ]
    for load in loads:
        load.start()

    x_at = lax.rem(lax.div(c, 2), 2) * 2 + lax.div(r, 4)
    xs_at = [lax.rem(x_at + n, 4) for n in range(4)]
    of_x = [4 * COLS * lax.rem(v, 2) + 2 * lax.div(v, 2) for v in xs_at]
    of_y = [COLS * lax.rem(lax.rem(r, 4) + n, 4) for n in range(4)]
    of_z = [4 * lax.rem(lax.div(c, 4) + n, 4) for n in range(4)]
    own_core = lax.rem(c, 2)
    other_core = 1 - 2 * own_core
    own_hi = 2 * lax.rem(lax.div(c, 2), 2)
    of_hi = [own_hi, 2 - own_hi]

    def for_all(visit):
        for hops in sorted(itertools.product(range(3), repeat=3), key=lambda h: -sum(h)):
            ones = [axis for axis in range(3) if hops[axis] == 1]

            def go(t, _):
                def pick(options, axis):
                    if axis not in ones:
                        return options[hops[axis]]
                    sign = lax.rem(lax.div(t, 2 ** (1 + ones.index(axis))), 2)
                    return options[1] + sign * (options[3] - options[1])

                core = own_core + lax.rem(t, 2) * other_core
                visit((pick(of_x, 0) + pick(of_y, 1)) + (pick(of_z, 2) + core))
                return 0

            lax.fori_loop(0 if sum(hops) else 1, 2 ** (1 + len(ones)), go, 0, unroll=True)

    def for_cols(visit, cores=2):
        for hi, z in ((1, 2), (1, 1), (1, 3), (0, 2), (1, 0), (0, 1), (0, 3), (0, 0)):

            def go(t, _):
                visit(of_hi[hi] + of_z[z] + (own_core + t * other_core))
                return 0

            if hi + z:
                lax.fori_loop(0, cores, go, 0, unroll=True)
            elif cores == 2:
                go(1, 0)

    def send_all(src, dst, sems):
        def visit(d):
            pltpu.make_async_remote_copy(
                src(d), dst, sems.at[0], sems.at[1], device_id=d, device_id_type=LOGICAL
            ).start()

        for_all(visit)

    def send_cols(src, dst, sems, cores=2):
        def visit(d):
            pltpu.make_async_remote_copy(
                src(d), dst, sems.at[0], sems.at[1], device_id=r * COLS + d, device_id_type=LOGICAL
            ).start()

        for_cols(visit, cores)

    def greet(d):
        pl.semaphore_signal(barrier, inc=1, device_id=d, device_id_type=LOGICAL)

    for_all(greet)

    def waiter(view, sems):
        return pltpu.make_async_remote_copy(view, view, sems.at[0], sems.at[1], device_id=(r, c), device_id_type=MESH)

    for load in loads[:3]:
        load.wait()
    pair_flat = pair_ref.reshape(POS, C)
    u = jnp.concatenate(
        [
            jnp.concatenate([pair_flat[pl.ds(4 * q + g, TI, stride=TJ)] for g in range(4)], axis=0).T
            for q in range(4)
        ],
        axis=1,
    )
    xhat, scale = norm(u)
    xhat_t[...] = xhat
    scale_t[...] = jnp.broadcast_to(scale, (8, POS))
    gain = jnp.broadcast_to(gain_first[...], (C, C)).T
    w03 = w_first[:, : 4 * C] * jnp.concatenate([gain] * 4, axis=1)
    w03_s[0] = left3(w03[:, : 2 * C])
    w03_s[1] = left3(w03[:, 2 * C :])
    proj = dot(left3(turn(w03)), right3(xhat))
    pos = lax.broadcasted_iota(jnp.int32, (8, POS), 1)
    in_row = (r * TI + pos % TI) < valid
    in_col = (c * TJ + pos // TI) < valid
    mask_t[...] = jnp.where(in_row & in_col, 1.0, 0.0).astype(F32)
    mask = mask_t[0:1]
    sig0 = jax.nn.sigmoid(proj[:C])
    sig2 = jax.nn.sigmoid(proj[2 * C : 3 * C])
    p1 = proj[C : 2 * C]
    p3 = proj[3 * C :]
    proj_t[0] = sig0
    proj_t[1] = p1
    proj_t[2] = sig2
    proj_t[3] = p3
    left = mask * sig0 * p1
    right = mask * sig2 * p3
    sa = send_a.reshape(N * 8, C)
    sb = send_b.reshape(N * 8, C)
    for q in range(4):
        sa[pl.ds(q, C, stride=8)] = left[:, 128 * q : 128 * (q + 1)]
        sb[pl.ds(q, C, stride=8)] = right[:, 128 * q : 128 * (q + 1)]


    pl.semaphore_wait(barrier, N - 1)
    send_all(lambda d: send_b.at[d, pl.ds(0, 4)], recv_b.at[me, pl.ds(0, 4)], b_sems)
    recv_b[me] = send_b[me]
    send_all(lambda d: send_a.at[d, pl.ds(0, 4)], recv_a.at[me, pl.ds(0, 4)], a_sems)
    recv_a[me] = send_a[me]

    pair_view = pair_ref.reshape(OWN, TJ, TJ, C)

    send_cols(lambda d: bias_any, bias_r.at[:, here], bias_sems, cores=1)
    send_cols(lambda d: pair_view.at[:, d], pair_r.at[:, here], pair_sems)
    pair_r[:, here] = pair_view[:, c]

    for load in loads[3:5] + loads[6:9]:
        load.wait()
    w4 = w_first[:, 4 * C :] * gain
    w4_s[...] = left3(w4)
    w4t_s[...] = left3(w4.T)
    w_m = w_mid[...] * jnp.broadcast_to(gain_mid[...], (C, C)).T
    wm_s[...] = left3(w_m)
    wmt_s[...] = left3(w_m.T)
    wo_s[...] = left3(w_att_out[...])
    wot_s[...] = left3(w_att_out[...].T)
    w_sec = w_second[...] * jnp.concatenate([jnp.broadcast_to(gain_second[...], (C, C)).T] * 4, axis=1)
    w2_s[...] = left3(w_sec)
    w2t_s[...] = left3(turn(w_sec))

    def factor(landing, sems, dest):
        waiter(landing.at[pl.ds(0, N - 1), pl.ds(0, 4)], sems).wait_recv()
        ra = landing.reshape(N * 8, C)
        for half in range(2):
            for q in range(4):
                ys = swap_blocks([ra[pl.ds((64 * half + 16 * rr) * 8 + q, COLS, stride=8)] for rr in range(4)])
                for g in range(4):
                    dest[pl.ds((4 * q + g) * COLS, COLS), pl.ds(128 * half, 128)] = ys[g]
        return dest[...]

    bt_parts = split(factor(recv_b, b_sems, bt_s))
    bt_hi[...], bt_lo[...] = bt_parts
    at = factor(recv_a, a_sems, at_s)
    a_parts = split(turn(at))
    at_hi[...], at_lo[...] = split(at)
    x = mm(a_parts, bt_parts)
    sx = send_x.reshape(N * 8, C)
    for l in range(OWN):
        for rr in range(ROWS):
            for jh in range(2):
                sx[pl.ds(16 * rr * 8 + 2 * l + jh, COLS, stride=8)] = x[
                    TI * rr + 16 * l : TI * rr + 16 * (l + 1), 128 * jh : 128 * (jh + 1)
                ]
    send_all(lambda d: send_x.at[d, pl.ds(0, 4)], recv_x.at[me, pl.ds(0, 4)], x_sems)
    recv_x[me] = send_x[me]

    send_cols(lambda d: cot_view.at[:, d], cot_r.at[:, here], cot_sems)
    half_bias = COLS // 2 - 1
    waiter(bias_r.reshape(HEADS * T, T).at[pl.ds(0, HEADS * TJ * half_bias)], bias_sems).wait_recv()
    loads[5].wait()
    odd = lax.rem(c, 2)
    bias_view = bias_r.reshape(HEADS, COLS // 2, 2, TJ, T)
    pltpu.make_async_remote_copy(
        bias_view.at[:, :, odd],
        bias_view.at[:, :, odd],
        twin_sems.at[0],
        twin_sems.at[1],
        device_id=(r, c + 1 - 2 * odd),
        device_id_type=MESH,
    ).start()
    waiter(pair_r.reshape(OWN * T, C).at[pl.ds(0, OWN * TJ * (COLS - 1))], pair_sems).wait_recv()
    pair_t = turn(pair_r.reshape(OWN * T, C)[...])
    ph, ps = norm(pair_t)
    g1 = jax.nn.sigmoid(dot(w4t_s[...], right3(ph)))
    waiter(recv_x.at[pl.ds(0, N - 1), pl.ds(0, 4)], x_sems).wait_recv()
    rx = recv_x.reshape(N * 8, C)
    x = jnp.concatenate([rx[pl.ds(m, C, stride=8)] for m in range(4)], axis=1)
    xh, xs = norm(x)
    m = dot(wmt_s[...], right3(xh))
    z1 = pair_t + g1 * m
    zh, zs = norm(z1)
    second = dot(w2t_s[...], right3(zh))
    score_scale = 1.0 / math.sqrt(WIDTH)
    qt_hi, qt_lo = split(second[:C] * score_scale)
    kt_hi, kt_lo = split(second[C : 2 * C])
    vt_hi, vt_lo = split(second[2 * C : 3 * C])
    g2 = jax.nn.sigmoid(second[3 * C :])
    waiter(bias_r.reshape(HEADS * T, T).at[pl.ds(0, HEADS * T // 2)], twin_sems).wait_recv()
    key = lax.broadcasted_iota(jnp.int32, (T, T), 0)
    shift = jnp.where(key < valid, 0.0, -MASK_SHIFT).astype(F32)
    for h in range(HEADS):
        bias_t[h] = bias_r[h].T + shift

    ots = [[], []]
    inverses = [[], []]
    all_keys = [head_keys(turn(second[C : 2 * C, T * l : T * (l + 1)])) for l in range(OWN)]
    for h in range(HEADS):
        hs = slice(WIDTH * h, WIDTH * (h + 1))
        for l in range(OWN):
            js = slice(T * l, T * (l + 1))
            keys = all_keys[l]
            s = dot(keys[h], head_queries(qt_hi[:, js], qt_lo[:, js], h)) + bias_t[h]
            e = jnp.exp(s - jnp.max(s, axis=0, keepdims=True))
            inverse = 1.0 / jnp.sum(e, axis=0, keepdims=True)
            eh, el = split(e)
            e_s[l, h] = e
            e_hi[l, h] = eh
            e_lo[l, h] = el
            both = dot(jnp.concatenate([vt_hi[hs, js], vt_lo[hs, js]], axis=0), eh)
            ots[l].append((both[:WIDTH] + (both[WIDTH:] + dot(vt_hi[hs, js], el))) * inverse)
            inverses[l].append(inverse)
    o = jnp.concatenate([jnp.concatenate(ots[l], axis=0) for l in range(OWN)], axis=1)

    out_flat = out_r.reshape(OWN * T, C)
    out_flat[...] = turn(z1 + dot(wot_s[...], right3(g2 * o)))
    out_view = out_ref.reshape(OWN, TJ, TJ, C)
    send_cols(lambda d: out_r.at[:, pl.ds(pl.multiple_of(d * TJ, TJ), TJ)], out_view.at[:, c], out_sems)
    out_view[:, c] = out_r[:, here]

    for load in loads[9:]:
        load.wait()
    waiter(cot_r.reshape(OWN * T, C).at[pl.ds(0, OWN * TJ * (COLS - 1))], cot_sems).wait_recv()
    cot = turn(cot_r.reshape(OWN * T, C)[...])
    dgated = dot(wo_s[...], right3(cot))
    d_o = dgated * g2
    d_s = dgated * o * g2 * (1.0 - g2)
    dqs = [[], []]
    dks = [[], []]
    dvs = [[], []]
    all_values = [head_keys(turn(second[2 * C : 3 * C, T * l : T * (l + 1)])) for l in range(OWN)]
    for h in range(HEADS):
        hs = slice(WIDTH * h, WIDTH * (h + 1))
        for l in range(OWN):
            js = slice(T * l, T * (l + 1))
            values = all_values[l]
            part = d_o[hs, js] * inverses[l][h]
            delta = jnp.sum(part * ots[l][h], axis=0, keepdims=True)
            dt_hi, dt_lo = split(part)
            zero = jnp.zeros_like(dt_hi)
            blocks = [None] * HEADS
            for n, block in enumerate((dt_hi, dt_lo, dt_hi, zero)):
                blocks[(h + n) % HEADS] = block
            dp = dot(values[h], jnp.concatenate(blocks, axis=0))
            dsh, dsl = split(e_s[l, h] * (dp - delta))
            both = dot(jnp.concatenate([kt_hi[hs, js], kt_lo[hs, js]], axis=0), dsh)
            dqs[l].append(both[:WIDTH] + (both[WIDTH:] + dot(kt_hi[hs, js], dsl)))
            both = dot(jnp.concatenate([qt_hi[hs, js], qt_lo[hs, js]], axis=0), dsh, NT)
            dks[l].append(both[:WIDTH] + (both[WIDTH:] + dot(qt_hi[hs, js], dsl, NT)))
            both = dot(jnp.concatenate([dt_hi, dt_lo], axis=0), e_hi[l, h], NT)
            dvs[l].append(both[:WIDTH] + (both[WIDTH:] + dot(dt_hi, e_lo[l, h], NT)))

    def stack(parts):
        return jnp.concatenate([jnp.concatenate(parts[l], axis=0) for l in range(OWN)], axis=1)

    d_second = jnp.concatenate([stack(dqs) * score_scale, stack(dks), stack(dvs), d_s], axis=0)
    dz1 = cot + norm_back(dot(w2_s[...], right3(d_second)), zh, zs)
    dx = norm_back(dot(wm_s[...], right3(dz1 * g1)), xh, xs)
    sd = send_d.reshape(N * 8, C)
    for n in range(4):
        sd[pl.ds(n, C, stride=8)] = dx[:, 128 * n : 128 * (n + 1)]
    send_all(lambda d: send_d.at[d, pl.ds(0, 4)], recv_d.at[me, pl.ds(0, 4)], d_sems)
    recv_d[me] = send_d[me]

    grad_part = grad_r.reshape(OWN * T, C)
    dp4 = dz1 * m * g1 * (1.0 - g1)
    grad_part[...] = turn(dz1 + norm_back(dot(w4_s[...], right3(dp4)), ph, ps))
    grad_view = grad_t.reshape(OWN, TJ, TJ, C)
    send_cols(lambda d: grad_r.at[:, pl.ds(pl.multiple_of(d * TJ, TJ), TJ)], grad_view.at[:, c], grad_sems)
    grad_view[:, c] = grad_r[:, here]

    waiter(recv_d.at[pl.ds(0, N - 1), pl.ds(0, 4)], d_sems).wait_recv()
    rd = recv_d.reshape(N * 8, C)
    for l in range(OWN):
        for rr in range(ROWS):
            for jh in range(2):
                dx_s[pl.ds(TI * rr + 16 * l, 16), pl.ds(128 * jh, 128)] = rd[
                    pl.ds(16 * rr * 8 + 2 * l + jh, COLS, stride=8)
                ]
    dx_parts = split(dx_s[...])

    def send_factor(d_src, buffer, landing, sems):
        sg = buffer.reshape(N * 8, C)
        for half in range(2):
            for q in range(4):
                ys = swap_blocks(
                    [
                        d_src[(4 * q + g) * COLS : (4 * q + g + 1) * COLS, 128 * half : 128 * (half + 1)]
                        for g in range(4)
                    ]
                )
                for rr in range(4):
                    sg[pl.ds((64 * half + 16 * rr) * 8 + q, COLS, stride=8)] = ys[rr]
        send_all(lambda d: buffer.at[d, pl.ds(0, 4)], landing.at[me, pl.ds(0, 4)], sems)
        landing[me] = buffer[me]

    send_factor(mm((at_hi[...], at_lo[...]), dx_parts), send_gb, recv_gb, gb_sems)
    send_factor(mm((bt_hi[...], bt_lo[...]), dx_parts, NT), send_ga, recv_ga, ga_sems)

    def factor_back(n, landing, sems):
        waiter(landing.at[pl.ds(0, N - 1), pl.ds(0, 4)], sems).wait_recv()
        rg = landing.reshape(N * 8, C)
        d = jnp.concatenate([rg[pl.ds(q, C, stride=8)] for q in range(4)], axis=1) * mask_t[0:1]
        gate = proj_t[n]
        d_value = d * gate
        d_gate = d_value * proj_t[n + 1] * (1.0 - gate)
        return dot(w03_s[n // 2], right3(jnp.concatenate([d_gate, d_value], axis=0)))

    du = factor_back(2, recv_gb, gb_sems)
    du = du + factor_back(0, recv_ga, ga_sems)
    res = turn(norm_back(du, xhat_t[...], scale_t[0:1]))
    grad_flat = grad_ref.reshape(POS, C)
    part_flat = grad_t.reshape(POS, C)
    waiter(grad_t.at[pl.ds(0, OWN * (COLS - 1))], grad_sems).wait_recv()
    for kk in range(TJ):
        grad_flat[pl.ds(kk, TI, stride=TJ)] = res[TI * kk : TI * (kk + 1)] + part_flat[pl.ds(kk, TI, stride=TJ)]

    waiter(recv_a.at[pl.ds(0, N - 1), pl.ds(0, 4)], a_sems).wait_send()
    waiter(recv_b.at[pl.ds(0, N - 1), pl.ds(0, 4)], b_sems).wait_send()
    waiter(pair_r.reshape(OWN * T, C).at[pl.ds(0, OWN * TJ * (COLS - 1))], pair_sems).wait_send()
    waiter(cot_r.reshape(OWN * T, C).at[pl.ds(0, OWN * TJ * (COLS - 1))], cot_sems).wait_send()
    waiter(bias_r.reshape(HEADS * T, T).at[pl.ds(0, HEADS * TJ * half_bias)], bias_sems).wait_send()
    waiter(bias_r.reshape(HEADS * T, T).at[pl.ds(0, HEADS * T // 2)], twin_sems).wait_send()
    waiter(recv_ga.at[pl.ds(0, N - 1), pl.ds(0, 4)], ga_sems).wait_send()
    waiter(recv_gb.at[pl.ds(0, N - 1), pl.ds(0, 4)], gb_sems).wait_send()
    waiter(recv_x.at[pl.ds(0, N - 1), pl.ds(0, 4)], x_sems).wait_send()
    waiter(recv_d.at[pl.ds(0, N - 1), pl.ds(0, 4)], d_sems).wait_send()
    waiter(grad_t.at[pl.ds(0, OWN * (COLS - 1))], grad_sems).wait_send()
    waiter(out_ref.at[pl.ds(0, OWN * (COLS - 1))], out_sems).wait()


def store(out_ref, grad_ref, out_any, grad_any, sems):
    copies = [
        pltpu.make_async_copy(out_ref, out_any, sems.at[0]),
        pltpu.make_async_copy(grad_ref, grad_any, sems.at[1]),
    ]
    for copy in copies:
        copy.start()
    for copy in copies:
        copy.wait()


def body(pair, cotangent, tri_bias, valid_length, gain_first, w_first, gain_mid, w_mid, gain_second, w_second, w_att_out):
    vmem = pl.BlockSpec(memory_space=pltpu.VMEM)
    smem = pl.BlockSpec(memory_space=pltpu.SMEM)
    hbm = pl.BlockSpec(memory_space=pltpu.HBM)
    tile = pltpu.VMEM((TI, TJ, C), F32)
    message = pltpu.VMEM((N, 8, C), F32)
    weight = pltpu.VMEM((C, 3 * C), BF16)
    rows = pltpu.VMEM((OWN, T, C), F32)
    square = pltpu.VMEM((T, T), F32)
    square_low = pltpu.VMEM((T, T), BF16)
    pair_of = pltpu.SemaphoreType.DMA((2,))
    results = pl.pallas_call(
        kernel,
        out_shape=(tile, tile),
        in_specs=[smem] + [hbm] * 10,
        out_specs=(vmem, vmem),
        scratch_shapes=[
            message,
            message,
            message,
            message,
            message,
            message,
            message,
            message,
            message,
            message,
            message,
            message,
            rows,
            rows,
            pltpu.VMEM((HEADS, T, T), F32),
            pltpu.VMEM((HEADS, T, T), F32),
            rows,
            rows,
            pltpu.VMEM((TI, TJ, C), F32),
            pltpu.VMEM((C, POS), F32),
            pltpu.VMEM((8, POS), F32),
            pltpu.VMEM((4, C, POS), F32),
            pltpu.VMEM((8, POS), F32),
            square,
            square,
            square_low,
            square_low,
            square_low,
            square_low,
            square,
            pltpu.VMEM((OWN, HEADS, T, T), F32),
            pltpu.VMEM((OWN, HEADS, T, T), BF16),
            pltpu.VMEM((OWN, HEADS, T, T), BF16),
            pltpu.VMEM((2, C, 6 * C), BF16),
            weight,
            weight,
            weight,
            weight,
            weight,
            weight,
            pltpu.VMEM((C, 12 * C), BF16),
            pltpu.VMEM((4 * C, 3 * C), BF16),
            pltpu.VMEM((TI, TJ, C), F32),
            pltpu.VMEM((C, 5 * C), F32),
            pltpu.VMEM((C, C), F32),
            pltpu.VMEM((C, 4 * C), F32),
            pltpu.VMEM((C, C), F32),
            pltpu.VMEM((1, C), F32),
            pltpu.VMEM((1, C), F32),
            pltpu.VMEM((1, C), F32),
            pltpu.SemaphoreType.DMA((10,)),
            pair_of,
            pair_of,
            pair_of,
            pair_of,
            pair_of,
            pair_of,
            pair_of,
            pair_of,
            pair_of,
            pair_of,
            pair_of,
            pair_of,
        ],
        compiler_params=pltpu.CompilerParams(
            collective_id=0, has_side_effects=True, vmem_limit_bytes=48 * 1024 * 1024
        ),
        cost_estimate=pl.CostEstimate(flops=2_000_000_000, bytes_accessed=4_000_000, transcendentals=1_000_000),
    )(
        valid_length,
        *(
            pltpu.with_memory_space_constraint(operand, pltpu.HBM)
            for operand in (
                pair,
                cotangent,
                tri_bias,
                gain_first.reshape(1, C),
                w_first,
                gain_mid.reshape(1, C),
                w_mid,
                gain_second.reshape(1, C),
                w_second,
                w_att_out,
            )
        ),
    )
    whole = jax.ShapeDtypeStruct((TI, TJ, C), F32)
    anywhere = pl.BlockSpec(memory_space=pl.ANY)
    return pl.pallas_call(
        store,
        out_shape=(whole, whole),
        in_specs=[anywhere, anywhere],
        out_specs=(anywhere, anywhere),
        scratch_shapes=[pltpu.SemaphoreType.DMA((2,))],
        compiler_params=pltpu.CompilerParams(vmem_limit_bytes=16 * 1024 * 1024),
    )(*(pltpu.with_memory_space_constraint(result, pltpu.VMEM) for result in results))


def solution(mesh):
    return jax.shard_map(
        body,
        mesh=mesh,
        in_specs=(
            P("row", "col", None),
            P("row", "col", None),
            P(None, "col", None),
            P(),
            P(),
            P(),
            P(),
            P(),
            P(),
            P(),
            P(),
        ),
        out_specs=(P("row", "col", None), P("row", "col", None)),
        check_vma=False,
    )
```

```python
import itertools
import math

import jax
import jax.numpy as jnp
from jax import lax
from jax.experimental import pallas as pl
from jax.experimental.pallas import tpu as pltpu
from jax.sharding import PartitionSpec as P

EPSILON = 1e-05
MASK_SHIFT = 1000000000.0
MESH = pl.DeviceIdType.MESH
LOGICAL = pl.DeviceIdType.LOGICAL
F32 = jnp.float32
BF16 = jnp.bfloat16
NN = (((1,), (0,)), ((), ()))
NT = (((1,), (1,)), ((), ()))

T = 256
C = 128
HEADS = 4
WIDTH = 32
ROWS = 8
COLS = 16
N = ROWS * COLS
TI = T // ROWS
TJ = T // COLS
POS = TI * TJ
OWN = T // N


def split(x):
    hi = x.astype(BF16)
    return hi, (x - hi.astype(F32)).astype(BF16)


def dot(a, b, dims=NN):
    return lax.dot_general(a, b, dims, preferred_element_type=F32)


def mm(a, b, dims=NN):
    return dot(a[0], b[0], dims) + (dot(a[0], b[1], dims) + dot(a[1], b[0], dims))


def norm(u):
    centre = u - jnp.mean(u, axis=0, keepdims=True)
    scale = lax.rsqrt(jnp.mean(centre * centre, axis=0, keepdims=True) + EPSILON)
    return centre * scale, scale


def norm_back(d, xhat, scale):
    mean_d = jnp.mean(d, axis=0, keepdims=True)
    mean_dx = jnp.mean(d * xhat, axis=0, keepdims=True)
    return scale * (d - mean_d - xhat * mean_dx)


def left3(x):
    hi, lo = split(x)
    return jnp.concatenate([hi, lo, hi], axis=1)


def right3(x):
    hi, lo = split(x)
    return jnp.concatenate([hi, hi, lo], axis=0)


def turn(x):
    rows, cols = x.shape
    return jnp.concatenate(
        [
            jnp.concatenate([x[128 * i : 128 * (i + 1), 128 * j : 128 * (j + 1)].T for i in range(rows // 128)], axis=1)
            for j in range(cols // 128)
        ],
        axis=0,
    )


def swap_blocks(xs):
    block = lax.broadcasted_iota(jnp.int32, xs[0].shape, 1) // 32
    for bit in (2, 1):
        upper = (block & bit) != 0
        ys = list(xs)
        for s in range(4):
            if s & bit == 0:
                a, b = xs[s], xs[s | bit]
                ys[s] = jnp.where(upper, pltpu.roll(b, 32 * bit, 1), a)
                ys[s | bit] = jnp.where(upper, b, pltpu.roll(a, 128 - 32 * bit, 1))
        xs = ys
    return xs


def head_keys(x):
    hi = x.astype(BF16).astype(F32)
    again = pltpu.roll(hi, WIDTH, 1)
    lo = pltpu.roll(x - hi, 2 * WIDTH, 1)
    block = lax.broadcasted_iota(jnp.int32, x.shape, 1) // WIDTH
    return [
        jnp.where(block == h, hi, jnp.where(block == (h + 1) % HEADS, again, lo)).astype(BF16) for h in range(HEADS)
    ]


def head_queries(hi, lo, h):
    own = slice(WIDTH * h, WIDTH * (h + 1))
    blocks = [None] * HEADS
    blocks[h] = hi[own]
    blocks[(h + 1) % HEADS] = lo[own]
    blocks[(h + 2) % HEADS] = hi[own]
    blocks[(h + 3) % HEADS] = jnp.zeros_like(hi[own])
    return jnp.concatenate(blocks, axis=0)


def kernel(
    valid_ref,
    pair_any,
    cot_any,
    bias_any,
    gain_first_any,
    w_first_any,
    gain_mid_any,
    w_mid_any,
    gain_second_any,
    w_second_any,
    w_att_out_any,
    out_ref,
    grad_ref,
    send_a,
    recv_a,
    send_b,
    recv_b,
    send_x,
    recv_x,
    send_d,
    recv_d,
    send_ga,
    recv_ga,
    send_gb,
    recv_gb,
    pair_r,
    cot_r,
    bias_r,
    bias_t,
    out_r,
    grad_r,
    grad_t,
    xhat_t,
    scale_t,
    proj_t,
    mask_t,
    at_s,
    bt_s,
    at_hi,
    at_lo,
    bt_hi,
    bt_lo,
    dx_s,
    e_s,
    e_hi,
    e_lo,
    w03_s,
    w4_s,
    w4t_s,
    wm_s,
    wmt_s,
    wo_s,
    wot_s,
    w2_s,
    w2t_s,
    pair_ref,
    w_first,
    w_mid,
    w_second,
    w_att_out,
    gain_first,
    gain_mid,
    gain_second,
    load_sems,
    a_sems,
    b_sems,
    x_sems,
    d_sems,
    ga_sems,
    gb_sems,
    pair_sems,
    cot_sems,
    bias_sems,
    twin_sems,
    out_sems,
    grad_sems,
):
    r = lax.axis_index("row")
    c = lax.axis_index("col")
    me = r * COLS + c
    valid = valid_ref[0]

    barrier = pltpu.get_barrier_semaphore()

    here = pl.ds(pl.multiple_of(c * TJ, TJ), TJ)
    cot_view = cot_any.reshape(OWN, TJ, TJ, C)
    loads = [
        pltpu.make_async_copy(src, dst, load_sems.at[n])
        for n, (src, dst) in enumerate(
            (
                (pair_any, pair_ref),
                (w_first_any, w_first),
                (gain_first_any, gain_first),
                (gain_mid_any, gain_mid),
                (gain_second_any, gain_second),
                (bias_any, bias_r.at[:, here]),
                (w_second_any, w_second),
                (w_mid_any, w_mid),
                (w_att_out_any, w_att_out),
                (cot_view.at[:, c], cot_r.at[:, here]),
            )
        )
    ]
    for load in loads:
        load.start()

    x_at = lax.rem(lax.div(c, 2), 2) * 2 + lax.div(r, 4)
    xs_at = [lax.rem(x_at + n, 4) for n in range(4)]
    of_x = [4 * COLS * lax.rem(v, 2) + 2 * lax.div(v, 2) for v in xs_at]
    of_y = [COLS * lax.rem(lax.rem(r, 4) + n, 4) for n in range(4)]
    of_z = [4 * lax.rem(lax.div(c, 4) + n, 4) for n in range(4)]
    own_core = lax.rem(c, 2)
    other_core = 1 - 2 * own_core
    own_hi = 2 * lax.rem(lax.div(c, 2), 2)
    of_hi = [own_hi, 2 - own_hi]

    def for_all(visit):
        for hops in sorted(itertools.product(range(3), repeat=3), key=lambda h: -sum(h)):
            ones = [axis for axis in range(3) if hops[axis] == 1]

            def go(t, _):
                def pick(options, axis):
                    if axis not in ones:
                        return options[hops[axis]]
                    sign = lax.rem(lax.div(t, 2 ** (1 + ones.index(axis))), 2)
                    return options[1] + sign * (options[3] - options[1])

                core = own_core + lax.rem(t, 2) * other_core
                visit((pick(of_x, 0) + pick(of_y, 1)) + (pick(of_z, 2) + core))
                return 0

            lax.fori_loop(0 if sum(hops) else 1, 2 ** (1 + len(ones)), go, 0, unroll=True)

    def for_cols(visit, cores=2):
        for hi, z in ((1, 2), (1, 1), (1, 3), (0, 2), (1, 0), (0, 1), (0, 3), (0, 0)):

            def go(t, _):
                visit(of_hi[hi] + of_z[z] + (own_core + t * other_core))
                return 0

            if hi + z:
                lax.fori_loop(0, cores, go, 0, unroll=True)
            elif cores == 2:
                go(1, 0)

    def send_all(src, dst, sems):
        def visit(d):
            pltpu.make_async_remote_copy(
                src(d), dst, sems.at[0], sems.at[1], device_id=d, device_id_type=LOGICAL
            ).start()

        for_all(visit)

    def send_cols(src, dst, sems, cores=2):
        def visit(d):
            pltpu.make_async_remote_copy(
                src(d), dst, sems.at[0], sems.at[1], device_id=r * COLS + d, device_id_type=LOGICAL
            ).start()

        for_cols(visit, cores)

    def greet(d):
        pl.semaphore_signal(barrier, inc=1, device_id=d, device_id_type=LOGICAL)

    for_all(greet)

    def waiter(view, sems):
        return pltpu.make_async_remote_copy(view, view, sems.at[0], sems.at[1], device_id=(r, c), device_id_type=MESH)

    for load in loads[:3]:
        load.wait()
    pair_flat = pair_ref.reshape(POS, C)
    u = jnp.concatenate(
        [
            jnp.concatenate([pair_flat[pl.ds(4 * q + g, TI, stride=TJ)] for g in range(4)], axis=0).T
            for q in range(4)
        ],
        axis=1,
    )
    xhat, scale = norm(u)
    xhat_t[...] = xhat
    scale_t[...] = jnp.broadcast_to(scale, (8, POS))
    gain = jnp.broadcast_to(gain_first[...], (C, C)).T
    w03 = w_first[:, : 4 * C] * jnp.concatenate([gain] * 4, axis=1)
    w03_s[0] = left3(w03[:, : 2 * C])
    w03_s[1] = left3(w03[:, 2 * C :])
    proj = dot(left3(turn(w03)), right3(xhat))
    pos = lax.broadcasted_iota(jnp.int32, (8, POS), 1)
    in_row = (r * TI + pos % TI) < valid
    in_col = (c * TJ + pos // TI) < valid
    mask_t[...] = jnp.where(in_row & in_col, 1.0, 0.0).astype(F32)
    mask = mask_t[0:1]
    sig0 = jax.nn.sigmoid(proj[:C])
    sig2 = jax.nn.sigmoid(proj[2 * C : 3 * C])
    p1 = proj[C : 2 * C]
    p3 = proj[3 * C :]
    proj_t[0] = sig0
    proj_t[1] = p1
    proj_t[2] = sig2
    proj_t[3] = p3
    left = mask * sig0 * p1
    right = mask * sig2 * p3
    sa = send_a.reshape(N * 8, C)
    sb = send_b.reshape(N * 8, C)
    for q in range(4):
        sa[pl.ds(q, C, stride=8)] = left[:, 128 * q : 128 * (q + 1)]
        sb[pl.ds(q, C, stride=8)] = right[:, 128 * q : 128 * (q + 1)]


    pl.semaphore_wait(barrier, N - 1)
    send_all(lambda d: send_a.at[d, pl.ds(0, 4)], recv_a.at[me, pl.ds(0, 4)], a_sems)
    recv_a[me] = send_a[me]
    send_all(lambda d: send_b.at[d, pl.ds(0, 4)], recv_b.at[me, pl.ds(0, 4)], b_sems)
    recv_b[me] = send_b[me]

    pair_view = pair_ref.reshape(OWN, TJ, TJ, C)

    send_cols(lambda d: bias_any, bias_r.at[:, here], bias_sems, cores=1)
    send_cols(lambda d: pair_view.at[:, d], pair_r.at[:, here], pair_sems)
    pair_r[:, here] = pair_view[:, c]

    for load in loads[3:5] + loads[6:9]:
        load.wait()
    w4 = w_first[:, 4 * C :] * gain
    w4_s[...] = left3(w4)
    w4t_s[...] = left3(w4.T)
    w_m = w_mid[...] * jnp.broadcast_to(gain_mid[...], (C, C)).T
    wm_s[...] = left3(w_m)
    wmt_s[...] = left3(w_m.T)
    wo_s[...] = left3(w_att_out[...])
    wot_s[...] = left3(w_att_out[...].T)
    w_sec = w_second[...] * jnp.concatenate([jnp.broadcast_to(gain_second[...], (C, C)).T] * 4, axis=1)
    w2_s[...] = left3(w_sec)
    w2t_s[...] = left3(turn(w_sec))

    def factor(landing, sems, dest):
        waiter(landing.at[pl.ds(0, N - 1), pl.ds(0, 4)], sems).wait_recv()
        ra = landing.reshape(N * 8, C)
        for half in range(2):
            for q in range(4):
                ys = swap_blocks([ra[pl.ds((64 * half + 16 * rr) * 8 + q, COLS, stride=8)] for rr in range(4)])
                for g in range(4):
                    dest[pl.ds((4 * q + g) * COLS, COLS), pl.ds(128 * half, 128)] = ys[g]
        return dest[...]

    at = factor(recv_a, a_sems, at_s)
    a_parts = split(turn(at))
    at_hi[...], at_lo[...] = split(at)
    bt_parts = split(factor(recv_b, b_sems, bt_s))
    bt_hi[...], bt_lo[...] = bt_parts
    x = mm(a_parts, bt_parts)
    sx = send_x.reshape(N * 8, C)
    for l in range(OWN):
        for rr in range(ROWS):
            for jh in range(2):
                sx[pl.ds(16 * rr * 8 + 2 * l + jh, COLS, stride=8)] = x[
                    TI * rr + 16 * l : TI * rr + 16 * (l + 1), 128 * jh : 128 * (jh + 1)
                ]
    send_all(lambda d: send_x.at[d, pl.ds(0, 4)], recv_x.at[me, pl.ds(0, 4)], x_sems)
    recv_x[me] = send_x[me]

    send_cols(lambda d: cot_view.at[:, d], cot_r.at[:, here], cot_sems)
    half_bias = COLS // 2 - 1
    waiter(bias_r.reshape(HEADS * T, T).at[pl.ds(0, HEADS * TJ * half_bias)], bias_sems).wait_recv()
    loads[5].wait()
    odd = lax.rem(c, 2)
    bias_view = bias_r.reshape(HEADS, COLS // 2, 2, TJ, T)
    pltpu.make_async_remote_copy(
        bias_view.at[:, :, odd],
        bias_view.at[:, :, odd],
        twin_sems.at[0],
        twin_sems.at[1],
        device_id=(r, c + 1 - 2 * odd),
        device_id_type=MESH,
    ).start()
    waiter(pair_r.reshape(OWN * T, C).at[pl.ds(0, OWN * TJ * (COLS - 1))], pair_sems).wait_recv()
    pair_t = turn(pair_r.reshape(OWN * T, C)[...])
    ph, ps = norm(pair_t)
    g1 = jax.nn.sigmoid(dot(w4t_s[...], right3(ph)))
    waiter(recv_x.at[pl.ds(0, N - 1), pl.ds(0, 4)], x_sems).wait_recv()
    rx = recv_x.reshape(N * 8, C)
    x = jnp.concatenate([rx[pl.ds(m, C, stride=8)] for m in range(4)], axis=1)
    xh, xs = norm(x)
    m = dot(wmt_s[...], right3(xh))
    z1 = pair_t + g1 * m
    zh, zs = norm(z1)
    second = dot(w2t_s[...], right3(zh))
    score_scale = 1.0 / math.sqrt(WIDTH)
    qt_hi, qt_lo = split(second[:C] * score_scale)
    kt_hi, kt_lo = split(second[C : 2 * C])
    vt_hi, vt_lo = split(second[2 * C : 3 * C])
    g2 = jax.nn.sigmoid(second[3 * C :])
    waiter(bias_r.reshape(HEADS * T, T).at[pl.ds(0, HEADS * T // 2)], twin_sems).wait_recv()
    key = lax.broadcasted_iota(jnp.int32, (T, T), 0)
    shift = jnp.where(key < valid, 0.0, -MASK_SHIFT).astype(F32)
    for h in range(HEADS):
        bias_t[h] = bias_r[h].T + shift

    ots = [[], []]
    inverses = [[], []]
    all_keys = [head_keys(turn(second[C : 2 * C, T * l : T * (l + 1)])) for l in range(OWN)]
    for h in range(HEADS):
        hs = slice(WIDTH * h, WIDTH * (h + 1))
        for l in range(OWN):
            js = slice(T * l, T * (l + 1))
            keys = all_keys[l]
            s = dot(keys[h], head_queries(qt_hi[:, js], qt_lo[:, js], h)) + bias_t[h]
            e = jnp.exp(s - jnp.max(s, axis=0, keepdims=True))
            inverse = 1.0 / jnp.sum(e, axis=0, keepdims=True)
            eh, el = split(e)
            e_s[l, h] = e
            e_hi[l, h] = eh
            e_lo[l, h] = el
            both = dot(jnp.concatenate([vt_hi[hs, js], vt_lo[hs, js]], axis=0), eh)
            ots[l].append((both[:WIDTH] + (both[WIDTH:] + dot(vt_hi[hs, js], el))) * inverse)
            inverses[l].append(inverse)
    o = jnp.concatenate([jnp.concatenate(ots[l], axis=0) for l in range(OWN)], axis=1)

    out_flat = out_r.reshape(OWN * T, C)
    out_flat[...] = turn(z1 + dot(wot_s[...], right3(g2 * o)))
    out_view = out_ref.reshape(OWN, TJ, TJ, C)
    send_cols(lambda d: out_r.at[:, pl.ds(pl.multiple_of(d * TJ, TJ), TJ)], out_view.at[:, c], out_sems)
    out_view[:, c] = out_r[:, here]

    for load in loads[9:]:
        load.wait()
    waiter(cot_r.reshape(OWN * T, C).at[pl.ds(0, OWN * TJ * (COLS - 1))], cot_sems).wait_recv()
    cot = turn(cot_r.reshape(OWN * T, C)[...])
    dgated = dot(wo_s[...], right3(cot))
    d_o = dgated * g2
    d_s = dgated * o * g2 * (1.0 - g2)
    dqs = [[], []]
    dks = [[], []]
    dvs = [[], []]
    all_values = [head_keys(turn(second[2 * C : 3 * C, T * l : T * (l + 1)])) for l in range(OWN)]
    for h in range(HEADS):
        hs = slice(WIDTH * h, WIDTH * (h + 1))
        for l in range(OWN):
            js = slice(T * l, T * (l + 1))
            values = all_values[l]
            part = d_o[hs, js] * inverses[l][h]
            delta = jnp.sum(part * ots[l][h], axis=0, keepdims=True)
            dt_hi, dt_lo = split(part)
            zero = jnp.zeros_like(dt_hi)
            blocks = [None] * HEADS
            for n, block in enumerate((dt_hi, dt_lo, dt_hi, zero)):
                blocks[(h + n) % HEADS] = block
            dp = dot(values[h], jnp.concatenate(blocks, axis=0))
            dsh, dsl = split(e_s[l, h] * (dp - delta))
            both = dot(jnp.concatenate([kt_hi[hs, js], kt_lo[hs, js]], axis=0), dsh)
            dqs[l].append(both[:WIDTH] + (both[WIDTH:] + dot(kt_hi[hs, js], dsl)))
            both = dot(jnp.concatenate([qt_hi[hs, js], qt_lo[hs, js]], axis=0), dsh, NT)
            dks[l].append(both[:WIDTH] + (both[WIDTH:] + dot(qt_hi[hs, js], dsl, NT)))
            both = dot(jnp.concatenate([dt_hi, dt_lo], axis=0), e_hi[l, h], NT)
            dvs[l].append(both[:WIDTH] + (both[WIDTH:] + dot(dt_hi, e_lo[l, h], NT)))

    def stack(parts):
        return jnp.concatenate([jnp.concatenate(parts[l], axis=0) for l in range(OWN)], axis=1)

    d_second = jnp.concatenate([stack(dqs) * score_scale, stack(dks), stack(dvs), d_s], axis=0)
    dz1 = cot + norm_back(dot(w2_s[...], right3(d_second)), zh, zs)
    dx = norm_back(dot(wm_s[...], right3(dz1 * g1)), xh, xs)
    sd = send_d.reshape(N * 8, C)
    for n in range(4):
        sd[pl.ds(n, C, stride=8)] = dx[:, 128 * n : 128 * (n + 1)]
    send_all(lambda d: send_d.at[d, pl.ds(0, 4)], recv_d.at[me, pl.ds(0, 4)], d_sems)
    recv_d[me] = send_d[me]

    grad_part = grad_r.reshape(OWN * T, C)
    dp4 = dz1 * m * g1 * (1.0 - g1)
    grad_part[...] = turn(dz1 + norm_back(dot(w4_s[...], right3(dp4)), ph, ps))
    grad_view = grad_t.reshape(OWN, TJ, TJ, C)
    send_cols(lambda d: grad_r.at[:, pl.ds(pl.multiple_of(d * TJ, TJ), TJ)], grad_view.at[:, c], grad_sems)
    grad_view[:, c] = grad_r[:, here]

    waiter(recv_d.at[pl.ds(0, N - 1), pl.ds(0, 4)], d_sems).wait_recv()
    rd = recv_d.reshape(N * 8, C)
    for l in range(OWN):
        for rr in range(ROWS):
            for jh in range(2):
                dx_s[pl.ds(TI * rr + 16 * l, 16), pl.ds(128 * jh, 128)] = rd[
                    pl.ds(16 * rr * 8 + 2 * l + jh, COLS, stride=8)
                ]
    dx_parts = split(dx_s[...])

    def send_factor(d_src, buffer, landing, sems):
        sg = buffer.reshape(N * 8, C)
        for half in range(2):
            for q in range(4):
                ys = swap_blocks(
                    [
                        d_src[(4 * q + g) * COLS : (4 * q + g + 1) * COLS, 128 * half : 128 * (half + 1)]
                        for g in range(4)
                    ]
                )
                for rr in range(4):
                    sg[pl.ds((64 * half + 16 * rr) * 8 + q, COLS, stride=8)] = ys[rr]
        send_all(lambda d: buffer.at[d, pl.ds(0, 4)], landing.at[me, pl.ds(0, 4)], sems)
        landing[me] = buffer[me]

    send_factor(mm((at_hi[...], at_lo[...]), dx_parts), send_gb, recv_gb, gb_sems)
    send_factor(mm((bt_hi[...], bt_lo[...]), dx_parts, NT), send_ga, recv_ga, ga_sems)

    def factor_back(n, landing, sems):
        waiter(landing.at[pl.ds(0, N - 1), pl.ds(0, 4)], sems).wait_recv()
        rg = landing.reshape(N * 8, C)
        d = jnp.concatenate([rg[pl.ds(q, C, stride=8)] for q in range(4)], axis=1) * mask_t[0:1]
        gate = proj_t[n]
        d_value = d * gate
        d_gate = d_value * proj_t[n + 1] * (1.0 - gate)
        return dot(w03_s[n // 2], right3(jnp.concatenate([d_gate, d_value], axis=0)))

    du = factor_back(2, recv_gb, gb_sems)
    du = du + factor_back(0, recv_ga, ga_sems)
    res = turn(norm_back(du, xhat_t[...], scale_t[0:1]))
    grad_flat = grad_ref.reshape(POS, C)
    part_flat = grad_t.reshape(POS, C)
    waiter(grad_t.at[pl.ds(0, OWN * (COLS - 1))], grad_sems).wait_recv()
    for kk in range(TJ):
        grad_flat[pl.ds(kk, TI, stride=TJ)] = res[TI * kk : TI * (kk + 1)] + part_flat[pl.ds(kk, TI, stride=TJ)]

    waiter(recv_a.at[pl.ds(0, N - 1), pl.ds(0, 4)], a_sems).wait_send()
    waiter(recv_b.at[pl.ds(0, N - 1), pl.ds(0, 4)], b_sems).wait_send()
    waiter(pair_r.reshape(OWN * T, C).at[pl.ds(0, OWN * TJ * (COLS - 1))], pair_sems).wait_send()
    waiter(cot_r.reshape(OWN * T, C).at[pl.ds(0, OWN * TJ * (COLS - 1))], cot_sems).wait_send()
    waiter(bias_r.reshape(HEADS * T, T).at[pl.ds(0, HEADS * TJ * half_bias)], bias_sems).wait_send()
    waiter(bias_r.reshape(HEADS * T, T).at[pl.ds(0, HEADS * T // 2)], twin_sems).wait_send()
    waiter(recv_ga.at[pl.ds(0, N - 1), pl.ds(0, 4)], ga_sems).wait_send()
    waiter(recv_gb.at[pl.ds(0, N - 1), pl.ds(0, 4)], gb_sems).wait_send()
    waiter(recv_x.at[pl.ds(0, N - 1), pl.ds(0, 4)], x_sems).wait_send()
    waiter(recv_d.at[pl.ds(0, N - 1), pl.ds(0, 4)], d_sems).wait_send()
    waiter(grad_t.at[pl.ds(0, OWN * (COLS - 1))], grad_sems).wait_send()
    waiter(out_ref.at[pl.ds(0, OWN * (COLS - 1))], out_sems).wait()


def store(out_ref, grad_ref, out_any, grad_any, sems):
    copies = [
        pltpu.make_async_copy(out_ref, out_any, sems.at[0]),
        pltpu.make_async_copy(grad_ref, grad_any, sems.at[1]),
    ]
    for copy in copies:
        copy.start()
    for copy in copies:
        copy.wait()


def body(pair, cotangent, tri_bias, valid_length, gain_first, w_first, gain_mid, w_mid, gain_second, w_second, w_att_out):
    vmem = pl.BlockSpec(memory_space=pltpu.VMEM)
    smem = pl.BlockSpec(memory_space=pltpu.SMEM)
    hbm = pl.BlockSpec(memory_space=pltpu.HBM)
    tile = pltpu.VMEM((TI, TJ, C), F32)
    message = pltpu.VMEM((N, 8, C), F32)
    weight = pltpu.VMEM((C, 3 * C), BF16)
    rows = pltpu.VMEM((OWN, T, C), F32)
    square = pltpu.VMEM((T, T), F32)
    square_low = pltpu.VMEM((T, T), BF16)
    pair_of = pltpu.SemaphoreType.DMA((2,))
    results = pl.pallas_call(
        kernel,
        out_shape=(tile, tile),
        in_specs=[smem] + [hbm] * 10,
        out_specs=(vmem, vmem),
        scratch_shapes=[
            message,
            message,
            message,
            message,
            message,
            message,
            message,
            message,
            message,
            message,
            message,
            message,
            rows,
            rows,
            pltpu.VMEM((HEADS, T, T), F32),
            pltpu.VMEM((HEADS, T, T), F32),
            rows,
            rows,
            pltpu.VMEM((TI, TJ, C), F32),
            pltpu.VMEM((C, POS), F32),
            pltpu.VMEM((8, POS), F32),
            pltpu.VMEM((4, C, POS), F32),
            pltpu.VMEM((8, POS), F32),
            square,
            square,
            square_low,
            square_low,
            square_low,
            square_low,
            square,
            pltpu.VMEM((OWN, HEADS, T, T), F32),
            pltpu.VMEM((OWN, HEADS, T, T), BF16),
            pltpu.VMEM((OWN, HEADS, T, T), BF16),
            pltpu.VMEM((2, C, 6 * C), BF16),
            weight,
            weight,
            weight,
            weight,
            weight,
            weight,
            pltpu.VMEM((C, 12 * C), BF16),
            pltpu.VMEM((4 * C, 3 * C), BF16),
            pltpu.VMEM((TI, TJ, C), F32),
            pltpu.VMEM((C, 5 * C), F32),
            pltpu.VMEM((C, C), F32),
            pltpu.VMEM((C, 4 * C), F32),
            pltpu.VMEM((C, C), F32),
            pltpu.VMEM((1, C), F32),
            pltpu.VMEM((1, C), F32),
            pltpu.VMEM((1, C), F32),
            pltpu.SemaphoreType.DMA((10,)),
            pair_of,
            pair_of,
            pair_of,
            pair_of,
            pair_of,
            pair_of,
            pair_of,
            pair_of,
            pair_of,
            pair_of,
            pair_of,
            pair_of,
        ],
        compiler_params=pltpu.CompilerParams(
            collective_id=0, has_side_effects=True, vmem_limit_bytes=48 * 1024 * 1024
        ),
        cost_estimate=pl.CostEstimate(flops=2_000_000_000, bytes_accessed=4_000_000, transcendentals=1_000_000),
    )(
        valid_length,
        *(
            pltpu.with_memory_space_constraint(operand, pltpu.HBM)
            for operand in (
                pair,
                cotangent,
                tri_bias,
                gain_first.reshape(1, C),
                w_first,
                gain_mid.reshape(1, C),
                w_mid,
                gain_second.reshape(1, C),
                w_second,
                w_att_out,
            )
        ),
    )
    whole = jax.ShapeDtypeStruct((TI, TJ, C), F32)
    anywhere = pl.BlockSpec(memory_space=pl.ANY)
    return pl.pallas_call(
        store,
        out_shape=(whole, whole),
        in_specs=[anywhere, anywhere],
        out_specs=(anywhere, anywhere),
        scratch_shapes=[pltpu.SemaphoreType.DMA((2,))],
        compiler_params=pltpu.CompilerParams(vmem_limit_bytes=16 * 1024 * 1024),
    )(*(pltpu.with_memory_space_constraint(result, pltpu.VMEM) for result in results))


def solution(mesh):
    return jax.shard_map(
        body,
        mesh=mesh,
        in_specs=(
            P("row", "col", None),
            P("row", "col", None),
            P(None, "col", None),
            P(),
            P(),
            P(),
            P(),
            P(),
            P(),
            P(),
            P(),
        ),
        out_specs=(P("row", "col", None), P("row", "col", None)),
        check_vma=False,
    )
```
